32 devices in a mesh: row: 8 (over z, x), col: 4 (over y, core).
Axes of the slice: x: 2, y: 2, z: 4, core: 2. Of those that a mesh axis runs over, the one named last changes fastest.
Arguments:
- homolog_tensor: bfloat16 [256, 128, 256], P('row', 'col'), may hold values from -6 to 6
- pairwise_tensor: bfloat16 [128, 128, 128], P('row', 'col'), may hold values from -6 to 6
- genuine_amino_flags: int32 [128], replicated, may hold values 0 or 1
- polymer_identity: int32 [128], replicated, may hold values from 0 to 3, never falling along the last dimension, each value on 1 to 64 neighbouring positions
- asking_weights: bfloat16 [256, 256], replicated, may hold values from -0.375 to 0.375
- attend_sigmoid_weights: bfloat16 [256, 256], replicated, may hold values from -0.375 to 0.375
- lookup_content_weights: bfloat16 [256, 512], replicated, may hold values from -0.375 to 0.375
- attend_final_weights: bfloat16 [256, 256], replicated, may hold values from -0.375 to 0.375
- pairwise_logit_weights: bfloat16 [128, 8], replicated, may hold values from -20 to 20
- crosspolymer_offset: float32 [8], replicated, may hold values from -2 to 2
- outgoing_link_weights: bfloat16 [128, 256], replicated, may hold values from -0.5 to 0.5
- incoming_link_weights: bfloat16 [128, 256], replicated, may hold values from -0.5 to 0.5
- trimult_sigmoid_weights: bfloat16 [128, 128], replicated, may hold values from -0.5 to 0.5
- trimult_final_weights: bfloat16 [128, 128], replicated, may hold values from -0.5 to 0.5
Outputs:
- attended_homologs: bfloat16 [256, 128, 256], P('row', 'col')
- pair_output: bfloat16 [128, 128, 128], P('row', 'col')
The draws below stay inside these ranges and needn't reach their ends.
Inputs may be any that keep to these rules, and one draw needn't show every extreme that they name: `polymer_identity`: chain ids never fall along the residues; each chain has 1 to 64 residues and one has exactly that many.
All inputs are finite; a program needn't handle non-finite values.
Results may differ from the reference program's by a relative error of at most 0.0035.
The reference program's roundings to bfloat16 on the way count: a program that leaves them out, or rounds other values in their place, can miss the bound.
Values may be sent and summed in bfloat16 or wider, within the bound.
A program may use at most 64 MiB of HBM per device.

```python
import math
import jax
import jax.numpy as jnp
import numpy as np
from jax import lax

FEATURE_DEPTH = 256
CZ = 128
H = 8
DH = 32
AMINO_TOTAL = 128
HOMOLOG_TOTAL = 256
ALL_HEADS_SPAN = 256


def draw_pairwise_logit_weights(key, part):
    key = jax.random.fold_in(key, 11)
    base_draw = jnp.clip(jax.random.normal(key, (CZ, H), jnp.float32), -5.0, 5.0)
    return (base_draw * 0.12).astype(jnp.bfloat16)


def place_ends(array, rng, least, top_value):
    index_at = [jax.random.randint(jax.random.fold_in(rng, axis), (), 0, length) for axis, length in enumerate(array.shape)]
    main_axis = array.shape.index(max(array.shape))
    beside = index_at[:main_axis] + [(index_at[main_axis] + 1) % array.shape[main_axis]] + index_at[main_axis + 1:]
    return array.at[tuple(index_at)].set(least).at[tuple(beside)].set(top_value)


def shard_levels(key, dims, shards, least, top_value):
    def one(axis_at, parts):
        heights = jax.random.uniform(jax.random.fold_in(jax.random.fold_in(key, 6), axis_at), (parts,), jnp.float32, least / len(shards), top_value / len(shards))
        return jnp.repeat(jnp.exp(heights), dims[axis_at] // parts).reshape((-1,) + (1,) * (len(dims) - axis_at - 1))

    factor_of = one(*shards[0])
    for cut in shards[1:]:
        factor_of = factor_of * one(*cut)
    return factor_of


def length_profile(amount, total, most, lean):
    portions = [(1 << 20) // math.isqrt(grade ** lean) + 1 for grade in range(2, amount + 1)]
    rest, given = total - most - (amount - 1), [1] * (amount - 1)
    while rest > 0:
        movable = [i for i in range(amount - 1) if given[i] < most]
        whole, left = sum([portions[i] for i in movable]), rest
        for i in movable:
            addition = min(most - given[i], max(1, left * portions[i] // whole), rest)
            given[i] = given[i] + addition
            rest = rest - addition
    return np.array([most] + given)


def uneven_parts(key, amount, total, bound, slope):
    if amount == 2:
        one = jax.random.randint(key, (), max(1, total - bound), min(bound, total - 1) + 1)
        return jnp.stack([one, total - one])
    tallies = jnp.asarray(length_profile(amount, total, bound, slope), jnp.int32)
    twos = (amount - 1) // 2
    giver, taker = tallies[1:1 + 2 * twos:2], tallies[2:2 + 2 * twos:2]
    room = jnp.minimum(giver - 1, bound - taker)
    passed = jax.random.randint(jax.random.fold_in(key, 1), (twos,), 0, 1 << 20) % (room + 1)
    tallies = tallies.at[1:1 + 2 * twos:2].set(giver - passed).at[2:2 + 2 * twos:2].set(taker + passed)
    return tallies[jax.random.permutation(jax.random.fold_in(key, 2), amount)]


def scatter_about(stream_key, dims, scale, reach, cuts=(), kind=jnp.bfloat16):
    result = jax.random.normal(stream_key, dims, jnp.float32) * scale
    if len(cuts) > 0:
        result = shard_levels(stream_key, dims, cuts, -0.22, 0.18) * result
    return jnp.clip(result, min=-reach, max=reach).astype(kind)


def setup_inputs(seed: int = 0) -> dict:
    key_of = jax.random.split(jax.random.key(seed), 15)
    return {
        "homolog_tensor": scatter_about(key_of[0], (HOMOLOG_TOTAL, AMINO_TOTAL, FEATURE_DEPTH), 1.0, 6.0, ((0, 8), (1, 4))),
        "pairwise_tensor": scatter_about(key_of[1], (AMINO_TOTAL, AMINO_TOTAL, CZ), 1.0, 6.0, ((0, 8), (1, 4))),
        "genuine_amino_flags": place_ends((jax.random.randint(key_of[2], (AMINO_TOTAL,), 0, 8) < 7).astype(jnp.int32), jax.random.fold_in(key_of[2], 1), 0, 1),
        "polymer_identity": jnp.searchsorted(jnp.cumsum(uneven_parts(key_of[3], 4, AMINO_TOTAL, AMINO_TOTAL // 2, 0)), jnp.arange(AMINO_TOTAL), side="right").astype(jnp.int32),
        "asking_weights": scatter_about(key_of[4], (FEATURE_DEPTH, ALL_HEADS_SPAN), FEATURE_DEPTH ** -0.5, 0.375),
        "attend_sigmoid_weights": scatter_about(key_of[5], (FEATURE_DEPTH, ALL_HEADS_SPAN), FEATURE_DEPTH ** -0.5, 0.375),
        "lookup_content_weights": scatter_about(key_of[6], (FEATURE_DEPTH, 2 * ALL_HEADS_SPAN), FEATURE_DEPTH ** -0.5, 0.375),
        "attend_final_weights": scatter_about(key_of[7], (ALL_HEADS_SPAN, FEATURE_DEPTH), ALL_HEADS_SPAN ** -0.5, 0.375),
        "pairwise_logit_weights": draw_pairwise_logit_weights(jax.random.fold_in(key_of[14], 71), 0),
        "crosspolymer_offset": jnp.clip(jax.random.uniform(key_of[9], (H,), jnp.float32, -2.0, 2.0), -2.0, 2.0),
        "outgoing_link_weights": scatter_about(key_of[10], (CZ, 2 * CZ), CZ ** -0.5, 0.5),
        "incoming_link_weights": scatter_about(key_of[11], (CZ, 2 * CZ), CZ ** -0.5, 0.5),
        "trimult_sigmoid_weights": scatter_about(key_of[12], (CZ, CZ), CZ ** -0.5, 0.5),
        "trimult_final_weights": scatter_about(key_of[13], (CZ, CZ), CZ ** -0.5, 0.5),
    }


def standardize_features(tensor):
    tensor = tensor.astype(jnp.float32)
    center = tensor - lax.optimization_barrier(jnp.mean(tensor, axis=-1, keepdims=True))
    spread = lax.optimization_barrier(jnp.mean(center * center, axis=-1, keepdims=True))
    return center * lax.rsqrt(spread + 1e-05)

def reference(homolog_tensor, pairwise_tensor, genuine_amino_flags, polymer_identity, asking_weights, attend_sigmoid_weights, lookup_content_weights, attend_final_weights, pairwise_logit_weights, crosspolymer_offset, outgoing_link_weights, incoming_link_weights, trimult_sigmoid_weights, trimult_final_weights):
    standardized_homologs = standardize_features(homolog_tensor).astype(jnp.bfloat16)
    pair_norm = standardize_features(pairwise_tensor).astype(jnp.bfloat16)
    pair_bias = jnp.einsum('ijc,ch->hij', pair_norm.astype(jnp.float32), pairwise_logit_weights.astype(jnp.float32)).astype(jnp.bfloat16)
    cross_chain = (polymer_identity[:, None] != polymer_identity[None, :]).astype(jnp.float32)
    extra_bias = pair_bias.astype(jnp.float32) + crosspolymer_offset[:, None, None] * cross_chain[None]
    keep_keys = (genuine_amino_flags > 0)[None, None, :]

    def single_homolog(split_parts):
        raw_row, norm_row = split_parts
        queries = (jnp.dot(norm_row, asking_weights, preferred_element_type=jnp.float32) * DH ** (-0.5)).astype(jnp.bfloat16)
        key_value = jnp.dot(norm_row, lookup_content_weights, preferred_element_type=jnp.float32).astype(jnp.bfloat16)
        gate_activation = jax.nn.sigmoid(jnp.dot(norm_row, attend_sigmoid_weights, preferred_element_type=jnp.float32))
        q_heads = queries.reshape(AMINO_TOTAL, H, DH).astype(jnp.float32)
        k_heads = key_value[:, :H * DH].reshape(AMINO_TOTAL, H, DH).astype(jnp.float32)
        v_heads = key_value[:, H * DH:].reshape(AMINO_TOTAL, H, DH).astype(jnp.float32)
        scores = jnp.einsum('qhd,khd->hqk', q_heads, k_heads) + extra_bias
        scores = jnp.where(keep_keys, scores, -1000000000.0)
        peak_now = lax.optimization_barrier(jnp.max(scores, axis=-1, keepdims=True))
        exp_scores = jnp.exp(scores - peak_now)
        total_now = lax.optimization_barrier(jnp.sum(exp_scores, axis=-1))
        probs = lax.optimization_barrier(exp_scores.astype(jnp.bfloat16)).astype(jnp.float32)
        attended = jnp.einsum('hqk,khd->qhd', probs, v_heads) / jnp.transpose(total_now)[:, :, None]
        gated_output = (gate_activation * attended.reshape(AMINO_TOTAL, H * DH)).astype(jnp.bfloat16)
        return (raw_row.astype(jnp.float32) + jnp.dot(gated_output, attend_final_weights, preferred_element_type=jnp.float32)).astype(jnp.bfloat16)
    attended_homologs = lax.map(single_homolog, (homolog_tensor, standardized_homologs))
    mask_rows = genuine_amino_flags.astype(jnp.float32)[:, None, None]
    left_proj = jnp.dot(pair_norm, outgoing_link_weights, preferred_element_type=jnp.float32)
    right_proj = jnp.dot(pair_norm, incoming_link_weights, preferred_element_type=jnp.float32)
    left_tri = (mask_rows * jax.nn.sigmoid(left_proj[..., :CZ]) * left_proj[..., CZ:]).astype(jnp.bfloat16)
    right_tri = (mask_rows * jax.nn.sigmoid(right_proj[..., :CZ]) * right_proj[..., CZ:]).astype(jnp.bfloat16)
    product = jnp.einsum('kic,kjc->ijc', left_tri.astype(jnp.float32), right_tri.astype(jnp.float32))
    product_norm = standardize_features(product).astype(jnp.bfloat16)
    tri_gate = jax.nn.sigmoid(jnp.dot(pair_norm, trimult_sigmoid_weights, preferred_element_type=jnp.float32))
    update = jnp.dot(product_norm, trimult_final_weights, preferred_element_type=jnp.float32)
    pair_output = (pairwise_tensor.astype(jnp.float32) + tri_gate * update).astype(jnp.bfloat16)
    return (attended_homologs, pair_output)
```

```python
import functools

import jax
import jax.numpy as jnp
from jax import lax
from jax.experimental import pallas as pl
from jax.experimental.pallas import tpu as pltpu
from jax.sharding import PartitionSpec as P

MESH = pl.DeviceIdType.MESH
F32 = jnp.float32
BF16 = jnp.bfloat16


def dot(a, b, contract=((1,), (0,))):
    return lax.dot_general(a, b, (contract, ((), ())), preferred_element_type=F32)


def normalize(x, axis):
    center = x - jnp.mean(x, axis=axis, keepdims=True)
    spread = jnp.mean(center * center, axis=axis, keepdims=True)
    return center * lax.rsqrt(spread + 1e-05)


def lane_blocks(shape, width):
    return lax.broadcasted_iota(jnp.int32, shape, len(shape) - 1) // width


def shift_lanes(x, amount):
    amount = amount % x.shape[-1]
    return x if amount == 0 else pltpu.roll(x, amount, x.ndim - 1)


def fused(
    dims,
    x_ref,
    pair_ref,
    mask_ref,
    keep_ref,
    cross_ref,
    offset_ref,
    wq_ref,
    wg_ref,
    wkv_ref,
    wo_ref,
    edge_w_ref,
    tri_gate_w_ref,
    tri_out_w_ref,
    msa_out_ref,
    pair_out_ref,
    hx,
    hout,
    send,
    recv,
    psend,
    precv,
    zed,
    zprod,
    extra,
    pn_ref,
    x_send_sem,
    x_recv_sem,
    e_send_sem,
    e_recv_sem,
    p_send_sem,
    p_recv_sem,
    o_send_sem,
    o_recv_sem,
):
    rows, cols, heads, channels = dims
    count = rows * cols
    row = lax.axis_index("row")
    col = lax.axis_index("col")
    me = row * cols + col
    seqs, residues, depth = hx.shape[1:]
    total_res = cols * residues
    width = depth // heads
    pair_rows, pair_cols, cz = pair_ref.shape
    positions = pair_rows * pair_cols

    def other(step):
        peer = lax.rem(me + step, count)
        return peer // cols, lax.rem(peer, cols)

    barrier = pltpu.get_barrier_semaphore()

    def greet(step, carry):
        pl.semaphore_signal(barrier, inc=1, device_id=other(step), device_id_type=MESH)
        return carry

    lax.fori_loop(1, count, greet, 0)
    pl.semaphore_wait(barrier, count - 1)

    for step in range(1, cols):
        peer = lax.rem(col + step, cols)
        pltpu.make_async_remote_copy(
            src_ref=x_ref.at[pl.ds(peer * seqs, seqs)],
            dst_ref=hx.at[col],
            send_sem=x_send_sem,
            recv_sem=x_recv_sem,
            device_id=(row, peer),
            device_id_type=MESH,
        ).start()
    hx[pl.ds(col, 1)] = x_ref[pl.ds(col * seqs, seqs)][None]

    with jax.named_scope("pair_edges_and_bias"):
        pair = pair_ref[...].astype(F32).reshape(positions, cz)
        pn = normalize(pair, -1).astype(BF16)
        pn_ref[...] = pn
        proj = dot(edge_w_ref[...], pn, ((1,), (1,)))
        both = 2 * cz
        edge = mask_ref[...] * jax.nn.sigmoid(proj[:both]) * proj[both : 2 * both]
        half = positions // 2
        edge = edge.reshape(count, 8, positions)
        bias = proj[2 * both : 2 * both + 8]
        send[:, :16, :] = jnp.concatenate(
            [edge[:, :, :half], edge[:, :, half:]], axis=1
        ).astype(BF16)
        bias = jnp.concatenate([bias[:, :half], bias[:, half:]], axis=0).astype(BF16)
        send[:, 16:, :] = jnp.broadcast_to(bias[None], (count, 16, half))

    def push(step, carry):
        to_row, to_col = other(step)
        slot = to_row * cols + to_col
        pltpu.make_async_remote_copy(
            src_ref=send.at[slot],
            dst_ref=recv.at[me],
            send_sem=e_send_sem,
            recv_sem=e_recv_sem,
            device_id=(to_row, to_col),
            device_id_type=MESH,
        ).start()
        return carry

    lax.fori_loop(1, count, push, 0)
    recv[pl.ds(me, 1)] = send[pl.ds(me, 1)]

    def wait_all(ref, sem):
        part = ref.at[pl.ds(0, count - 1)]
        pltpu.make_async_copy(part, part, sem).wait()

    wait_all(recv, e_recv_sem)

    block = pair_cols
    lanes = total_res
    per_tile = lanes // block
    where_block = lane_blocks((16 * rows, lanes), block)
    with jax.named_scope("to_matrices"):
        for part in range(2):
            for tile in range(half // lanes):
                taken = recv[:, part * 16 : part * 16 + 16, tile * lanes : (tile + 1) * lanes]
                taken = taken.astype(F32).reshape(rows, cols, 16, lanes)
                pieces = [taken[:, c].reshape(16 * rows, lanes) for c in range(cols)]
                for k in range(per_tile):
                    merged = shift_lanes(pieces[0], (0 - k) * block)
                    for c in range(1, cols):
                        merged = jnp.where(
                            where_block == c, shift_lanes(pieces[c], (c - k) * block), merged
                        )
                    zed[part, pl.ds(tile * per_tile + k, 16 * rows, stride=8), :] = merged

    def matrix(part, q):
        return zed[part].reshape(2 * rows, 8, 8, lanes)[:, q].reshape(total_res, lanes)

    with jax.named_scope("triangle_product"):
        mine = channels // count
        for ch in range(mine):
            left = matrix(0, ch).T.astype(BF16)
            right = matrix(0, mine + ch).astype(BF16)
            product = dot(left, right).reshape(2 * rows, 8, lanes)
            zprod[:, ch] = product
        where_small = lane_blocks((2 * rows * mine, lanes), block)
        for tile in range(half // lanes):
            taken = [
                zprod.reshape(2 * rows * mine * 8, lanes)[
                    pl.ds(tile * per_tile + k, 2 * rows * mine, stride=8), :
                ]
                for k in range(per_tile)
            ]
            merged_all = []
            for c in range(cols):
                merged = shift_lanes(taken[0], (0 - c) * block)
                for k in range(1, per_tile):
                    merged = jnp.where(
                        where_small == k, shift_lanes(taken[k], (k - c) * block), merged
                    )
                merged_all.append(merged.reshape(rows, 2 * mine, lanes))
            psend[:, :, tile * lanes : (tile + 1) * lanes] = jnp.stack(
                merged_all, axis=1
            ).reshape(count, 2 * mine, lanes)

    def push_product(step, carry):
        to_row, to_col = other(step)
        slot = to_row * cols + to_col
        pltpu.make_async_remote_copy(
            src_ref=psend.at[slot],
            dst_ref=precv.at[me],
            send_sem=p_send_sem,
            recv_sem=p_recv_sem,
            device_id=(to_row, to_col),
            device_id_type=MESH,
        ).start()
        return carry

    lax.fori_loop(1, count, push_product, 0)
    precv[pl.ds(me, 1)] = psend[pl.ds(me, 1)]

    with jax.named_scope("attention_bias"):
        for h in range(heads):
            extra[h] = matrix(1, h) + offset_ref[h] * cross_ref[...]

    three = hx.at[pl.ds(0, cols - 1)]
    pltpu.make_async_copy(three, three, x_recv_sem).wait()

    keep = keep_ref[...] > 0
    head_of = lane_blocks((total_res, depth), width)

    def attend(s, carry):
        x = hx[:, s].reshape(total_res, depth).astype(F32)
        xn = normalize(x, -1).astype(BF16)
        queries = (dot(xn, wq_ref[...]) * width ** (-0.5)).astype(BF16)
        kv = dot(xn, wkv_ref[...])
        keys, values = kv[:, :depth], kv[:, depth:]
        gate = jax.nn.sigmoid(dot(xn, wg_ref[...]))
        key_stack = jnp.concatenate(
            [jnp.where(head_of == h, keys, 0.0).astype(BF16) for h in range(heads)], axis=0
        )
        value_stack = jnp.concatenate(
            [jnp.where(head_of == h, values, 0.0).astype(BF16) for h in range(heads)], axis=0
        )
        scores = dot(queries, key_stack, ((1,), (1,)))
        probs = []
        total = jnp.ones((total_res, depth), F32)
        for h in range(heads):
            one = scores[:, h * total_res : (h + 1) * total_res] + extra[h]
            one = jnp.where(keep, one, -1000000000.0)
            one = jnp.exp(one - jnp.max(one, axis=-1, keepdims=True))
            total = jnp.where(head_of == h, jnp.sum(one, axis=-1, keepdims=True), total)
            probs.append(one.astype(BF16))
        attended = dot(jnp.concatenate(probs, axis=1), value_stack) / total
        gated = (gate * attended).astype(BF16)
        result = (x + dot(gated, wo_ref[...])).astype(BF16)
        hout[:, s] = result.reshape(cols, residues, depth)
        for step in range(1, cols):
            peer = lax.rem(col + step, cols)
            pltpu.make_async_remote_copy(
                src_ref=hout.at[peer, s],
                dst_ref=msa_out_ref.at[col * seqs + s],
                send_sem=o_send_sem,
                recv_sem=o_recv_sem,
                device_id=(row, peer),
                device_id_type=MESH,
            ).start()
        msa_out_ref[pl.ds(col * seqs + s, 1)] = hout[pl.ds(col, 1), s]
        return carry

    with jax.named_scope("row_attention"):
        lax.fori_loop(0, seqs, attend, 0)

    wait_all(precv, p_recv_sem)
    with jax.named_scope("pair_update"):
        product = precv[...]
        in_half = lax.broadcasted_iota(jnp.int32, (8, half), 0) < mine

        def spread_halves(partial):
            low = jnp.sum(jnp.where(in_half, partial, 0.0), axis=0, keepdims=True)
            high = jnp.sum(jnp.where(in_half, 0.0, partial), axis=0, keepdims=True)
            return jnp.where(in_half, low, high) / channels

        center = product - spread_halves(jnp.sum(product, axis=0))[None]
        spread = spread_halves(jnp.sum(center * center, axis=0))
        norm = (center * lax.rsqrt(spread + 1e-05)[None]).reshape(count * 8, half)
        update = dot(norm.T.astype(BF16), tri_out_w_ref[...])
        update = jnp.concatenate([update[:, :cz], update[:, cz:]], axis=0)
        tri_gate = jax.nn.sigmoid(dot(pn_ref[...], tri_gate_w_ref[...]))
        pair = pair_ref[...].astype(F32).reshape(positions, cz)
        pair_out_ref[...] = (
            (pair + tri_gate * update).astype(BF16).reshape(pair_rows, pair_cols, cz)
        )

    pltpu.make_async_copy(three, three, x_send_sem).wait()
    wait_all(send, e_send_sem)
    wait_all(psend, p_send_sem)
    pltpu.make_async_copy(three, three, o_send_sem).wait()
    pltpu.make_async_copy(three, three, o_recv_sem).wait()


def local_fused(
    rows,
    cols,
    homolog_tensor,
    pairwise_tensor,
    genuine_amino_flags,
    polymer_identity,
    asking_weights,
    attend_sigmoid_weights,
    lookup_content_weights,
    attend_final_weights,
    pairwise_logit_weights,
    crosspolymer_offset,
    outgoing_link_weights,
    incoming_link_weights,
    trimult_sigmoid_weights,
    trimult_final_weights,
):
    count = rows * cols
    homologs, residues, depth = homolog_tensor.shape
    pair_rows, pair_cols, cz = pairwise_tensor.shape
    heads = pairwise_logit_weights.shape[1]
    total_res = cols * residues
    seqs = homologs // cols
    mine = cz // count
    half = pair_rows * pair_cols // 2
    row = lax.axis_index("row")
    flags = genuine_amino_flags.astype(F32)
    mask = lax.dynamic_slice_in_dim(flags, row * pair_rows, pair_rows, 0)
    mask = jnp.broadcast_to(mask[:, None], (pair_rows, pair_cols)).reshape(1, -1)
    cross = (polymer_identity[:, None] != polymer_identity[None, :]).astype(F32)
    by_owner = jnp.stack(
        [
            outgoing_link_weights.reshape(cz, 2, count, mine),
            incoming_link_weights.reshape(cz, 2, count, mine),
        ],
        axis=3,
    )
    edge_weights = jnp.concatenate(
        [
            jnp.transpose(by_owner, (1, 2, 3, 4, 0)).reshape(4 * cz, cz),
            jnp.transpose(pairwise_logit_weights),
            jnp.zeros((16 - heads, cz), BF16),
        ],
        axis=0,
    )
    final = trimult_final_weights.reshape(count, 1, mine, 1, cz)
    same_half = jnp.eye(2, dtype=BF16).reshape(1, 2, 1, 2, 1)
    tri_out = (final * same_half).reshape(count * 2 * mine, 2 * cz)
    vmem = pl.BlockSpec(memory_space=pltpu.VMEM)
    smem = pl.BlockSpec(memory_space=pltpu.SMEM)
    dma = pltpu.SemaphoreType.DMA
    return pl.pallas_call(
        functools.partial(fused, (rows, cols, heads, cz)),
        out_shape=(
            jax.ShapeDtypeStruct(homolog_tensor.shape, BF16),
            jax.ShapeDtypeStruct(pairwise_tensor.shape, BF16),
        ),
        in_specs=[vmem] * 5 + [smem] + [vmem] * 7,
        out_specs=(vmem, vmem),
        scratch_shapes=[
            pltpu.VMEM((cols, seqs, residues, depth), BF16),
            pltpu.VMEM((cols, seqs, residues, depth), BF16),
            pltpu.VMEM((count, 32, half), BF16),
            pltpu.VMEM((count, 32, half), BF16),
            pltpu.VMEM((count, 2 * mine, half), F32),
            pltpu.VMEM((count, 2 * mine, half), F32),
            pltpu.VMEM((2, 8 * total_res, total_res), F32),
            pltpu.VMEM((2 * rows, mine, 8, total_res), F32),
            pltpu.VMEM((heads, total_res, total_res), F32),
            pltpu.VMEM((pair_rows * pair_cols, cz), BF16),
        ]
        + [dma] * 8,
        compiler_params=pltpu.CompilerParams(
            collective_id=0, has_side_effects=True, vmem_limit_bytes=40 * 2**20
        ),
    )(
        homolog_tensor,
        pairwise_tensor,
        mask,
        flags.reshape(1, -1),
        cross,
        crosspolymer_offset,
        asking_weights,
        attend_sigmoid_weights,
        lookup_content_weights,
        attend_final_weights,
        edge_weights,
        trimult_sigmoid_weights,
        tri_out,
    )


def from_root(array, axis, root):
    mine = lax.axis_index(axis) == root
    return lax.psum(jnp.where(mine, array, jnp.zeros_like(array)), axis)


def standardize_features(tensor):
    tensor = tensor.astype(jnp.float32)
    center = tensor - jnp.mean(tensor, axis=-1, keepdims=True)
    spread = jnp.mean(center * center, axis=-1, keepdims=True)
    return center * lax.rsqrt(spread + 1e-05)


def edges(pair_norm, weight, mask_rows, width):
    projected = jnp.dot(pair_norm, weight, preferred_element_type=jnp.float32)
    edge_vals = (
        mask_rows * jax.nn.sigmoid(projected[..., :width]) * projected[..., width:]
    ).astype(jnp.bfloat16)
    return jnp.transpose(edge_vals, (2, 0, 1))


def local(
    homolog_tensor,
    pairwise_tensor,
    genuine_amino_flags,
    polymer_identity,
    asking_weights,
    attend_sigmoid_weights,
    lookup_content_weights,
    attend_final_weights,
    pairwise_logit_weights,
    crosspolymer_offset,
    outgoing_link_weights,
    incoming_link_weights,
    trimult_sigmoid_weights,
    trimult_final_weights,
):
    row_count = lax.axis_size("row")
    col_count = lax.axis_size("col")
    row_index = lax.axis_index("row")
    col_index = lax.axis_index("col")
    homolog_entries, amino_positions, feature_depth = homolog_tensor.shape
    res_rows = pairwise_tensor.shape[0]
    pair_width = pairwise_tensor.shape[2]
    row_ratio = row_count // col_count
    head_count = pairwise_logit_weights.shape[1]
    inner_width = asking_weights.shape[1]
    per_head_width = inner_width // head_count
    standardized_homologs = standardize_features(homolog_tensor).astype(jnp.bfloat16)
    pair_norm = standardize_features(pairwise_tensor).astype(jnp.bfloat16)
    local_bias = jnp.einsum(
        "ijc,ch->hij", pair_norm, pairwise_logit_weights, preferred_element_type=jnp.float32
    ).astype(jnp.bfloat16)
    row_bias = lax.all_gather(local_bias, "col", axis=2, tiled=True)
    queries = (
        jnp.dot(standardized_homologs, asking_weights, preferred_element_type=jnp.float32)
        * per_head_width ** (-0.5)
    ).astype(jnp.bfloat16)
    queries = queries.reshape(homolog_entries, amino_positions, head_count, per_head_width)
    gate_activation = jax.nn.sigmoid(
        jnp.dot(standardized_homologs, attend_sigmoid_weights, preferred_element_type=jnp.float32)
    )
    all_bias = lax.all_gather(row_bias, "row", axis=1, tiled=True)
    bias_block = lax.dynamic_slice_in_dim(all_bias, col_index * amino_positions, amino_positions, 1)
    query_chain = lax.dynamic_slice_in_dim(
        polymer_identity, col_index * amino_positions, amino_positions, 0
    )
    cross_chain = (query_chain[:, None] != polymer_identity[None, :]).astype(jnp.float32)
    extra_bias = (
        bias_block.astype(jnp.float32) + crosspolymer_offset[:, None, None] * cross_chain[None]
    )
    keep_all = genuine_amino_flags > 0
    key_value = jnp.dot(
        lax.all_gather(standardized_homologs, "col", axis=1, tiled=True),
        lookup_content_weights,
        preferred_element_type=jnp.float32,
    ).astype(jnp.bfloat16)
    piece_len = key_value.shape[1]
    key_rows = key_value[..., :inner_width].reshape(
        homolog_entries, piece_len, head_count, per_head_width
    )
    value_rows = key_value[..., inner_width:].reshape(
        homolog_entries, piece_len, head_count, per_head_width
    )
    scores = jnp.einsum("sqhd,skhd->shqk", queries, key_rows, preferred_element_type=jnp.float32)
    scores = scores + extra_bias[None]
    scores = jnp.where(keep_all, scores, -1000000000.0)
    peak_old = jnp.full((homolog_entries, head_count, amino_positions), -jnp.inf, jnp.float32)
    total_old = jnp.zeros((homolog_entries, head_count, amino_positions), jnp.float32)
    accum_old = jnp.zeros(
        (homolog_entries, head_count, amino_positions, per_head_width), jnp.float32
    )
    peak_now = jnp.max(scores, axis=-1)
    factor = jnp.exp(peak_old - peak_now)
    exp_scores = jnp.exp(scores - peak_now[..., None])
    total_now = total_old * factor + jnp.sum(exp_scores, axis=-1)
    accum_now = accum_old * factor[..., None] + jnp.einsum(
        "shqk,skhd->shqd",
        exp_scores.astype(jnp.bfloat16),
        value_rows,
        preferred_element_type=jnp.float32,
    )
    peak_now, total_now, accum_now = (peak_now, total_now, accum_now)
    attended = accum_now / total_now[..., None]
    attended = jnp.transpose(attended, (0, 2, 1, 3)).reshape(
        homolog_entries, amino_positions, inner_width
    )
    gated_output = (gate_activation * attended).astype(jnp.bfloat16)
    attended_homologs = (
        homolog_tensor.astype(jnp.float32)
        + jnp.dot(gated_output, attend_final_weights, preferred_element_type=jnp.float32)
    ).astype(jnp.bfloat16)
    mask_rows = lax.dynamic_slice_in_dim(
        genuine_amino_flags, row_index * res_rows, res_rows, 0
    ).astype(jnp.float32)[:, None, None]
    left_tri = edges(pair_norm, outgoing_link_weights, mask_rows, pair_width)
    right_tri = edges(pair_norm, incoming_link_weights, mask_rows, pair_width)
    left_cols = lax.all_gather(left_tri, "row", axis=1, tiled=True)
    left_part = lax.dynamic_slice_in_dim(left_cols, row_index % row_ratio * res_rows, res_rows, 2)
    left_mine = from_root(left_part, "col", row_index // row_ratio)
    product = jnp.einsum(
        "cki,ckj->cij",
        left_mine,
        lax.all_gather(right_tri, "row", axis=1, tiled=True),
        preferred_element_type=jnp.float32,
    )
    product_norm = standardize_features(jnp.transpose(product, (1, 2, 0))).astype(jnp.bfloat16)
    tri_gate = jax.nn.sigmoid(
        jnp.dot(pair_norm, trimult_sigmoid_weights, preferred_element_type=jnp.float32)
    )
    update = jnp.dot(product_norm, trimult_final_weights, preferred_element_type=jnp.float32)
    pair_output = (pairwise_tensor.astype(jnp.float32) + tri_gate * update).astype(jnp.bfloat16)
    return (attended_homologs, pair_output)


def solution(mesh):
    in_specs = (
        P("row", "col", None),
        P("row", "col", None),
        P(),
        P(),
        P(),
        P(),
        P(),
        P(),
        P(),
        P(),
        P(),
        P(),
        P(),
        P(),
    )
    out_specs = (P("row", "col", None), P("row", "col", None))

    def local_either(*blocks):
        rows, cols = mesh.shape["row"], mesh.shape["col"]
        homologs, residues, depth = blocks[0].shape
        pair_rows, pair_cols, cz = blocks[1].shape
        heads = blocks[8].shape[1]
        fits = (
            cz == 4 * rows * cols
            and cz == cols * residues
            and cz == rows * pair_rows
            and pair_cols == residues == 32
            and pair_rows == 16
            and heads == 8
            and homologs % cols == 0
            and blocks[4].shape[1] == depth
            and depth % 128 == 0
        )
        if fits:
            return local_fused(rows, cols, *blocks)
        return local(*blocks)

    return jax.shard_map(local_either, mesh=mesh, in_specs=in_specs, out_specs=out_specs, check_vma=False)
```

```python
import functools

import jax
import jax.numpy as jnp
from jax import lax
from jax.experimental import pallas as pl
from jax.experimental.pallas import tpu as pltpu
from jax.sharding import PartitionSpec as P

MESH = pl.DeviceIdType.MESH
F32 = jnp.float32
BF16 = jnp.bfloat16


def dot(a, b, contract=((1,), (0,))):
    return lax.dot_general(a, b, (contract, ((), ())), preferred_element_type=F32)


def normalize(x, axis):
    center = x - jnp.mean(x, axis=axis, keepdims=True)
    spread = jnp.mean(center * center, axis=axis, keepdims=True)
    return center * lax.rsqrt(spread + 1e-05)


def lane_blocks(shape, width):
    return lax.broadcasted_iota(jnp.int32, shape, len(shape) - 1) // width


def shift_lanes(x, amount):
    amount = amount % x.shape[-1]
    return x if amount == 0 else pltpu.roll(x, amount, x.ndim - 1)


def fused(
    dims,
    x_ref,
    pair_hbm,
    flags_smem,
    keep_ref,
    identity_ref,
    offset_ref,
    wq_hbm,
    wg_hbm,
    wkv_hbm,
    wo_hbm,
    bias_w_ref,
    left_w_hbm,
    right_w_hbm,
    tri_gate_w_hbm,
    tri_out_w_hbm,
    msa_out_ref,
    pair_out_ref,
    hx,
    hout,
    send,
    recv,
    brecv,
    psend,
    precv,
    zed,
    zprod,
    extra,
    pn_ref,
    q_ref,
    k_ref,
    v_ref,
    g_ref,
    pair_ref,
    wq_ref,
    wg_ref,
    wkv_ref,
    wo_ref,
    left_w_ref,
    right_w_ref,
    tri_gate_w_ref,
    tri_out_w_ref,
    in_sem,
    own_sem,
    x_send_sem,
    x_recv_sem,
    e_send_sem,
    e_recv_sem,
    p_send_sem,
    p_recv_sem,
    o_send_sem,
    o_recv_sem,
    r_send_sem,
    r_recv_sem,
    c_send_sem,
    c_recv_sem,
):
    rows, cols, heads, channels = dims
    count = rows * cols
    mine = channels // count
    row = lax.axis_index("row")
    col = lax.axis_index("col")
    me = row * cols + col
    seqs, residues, depth = hx.shape[1:]
    total_res = cols * residues
    width = depth // heads
    pair_rows, pair_cols, cz = pair_ref.shape
    positions = pair_rows * pair_cols
    half = positions // 2
    both = 2 * cz

    def other(step):
        peer = lax.rem(me + step, count)
        return peer // cols, lax.rem(peer, cols)

    barrier = pltpu.get_barrier_semaphore()

    def greet(step, carry):
        pl.semaphore_signal(barrier, inc=1, device_id=other(step), device_id_type=MESH)
        return carry

    loads = [
        pltpu.make_async_copy(source, target, in_sem.at[n])
        for n, (source, target) in enumerate(
            (
                (pair_hbm, pair_ref),
                (left_w_hbm, left_w_ref),
                (right_w_hbm, right_w_ref),
                (tri_out_w_hbm, tri_out_w_ref),
                (tri_gate_w_hbm, tri_gate_w_ref),
                (wq_hbm, wq_ref),
                (wkv_hbm, wkv_ref),
                (wg_hbm, wg_ref),
                (wo_hbm, wo_ref),
            )
        )
    ]
    for load in loads:
        load.start()
    own = pltpu.make_async_copy(x_ref.at[pl.ds(col * seqs, seqs)], hx.at[col], own_sem)
    own.start()
    lax.fori_loop(1, count, greet, 0)

    with jax.named_scope("weights_by_owner"):
        to = lax.broadcasted_iota(jnp.int32, (both, both), 0)
        source = lax.broadcasted_iota(jnp.int32, (both, both), 1)
        wanted = (to % (2 * mine)) // mine * cz + to // (2 * mine) * mine + to % mine
        order = (source == wanted).astype(BF16)
        loads[1].wait()
        loads[2].wait()
        edge_w = [
            dot(
                order,
                jnp.concatenate(
                    [left_w_ref[:, n * cz : n * cz + cz], right_w_ref[:, n * cz : n * cz + cz]],
                    axis=1,
                ),
                ((1,), (1,)),
            ).astype(BF16)
            for n in range(2)
        ]

    with jax.named_scope("pair_edges_and_bias"):
        loads[0].wait()
        pair = pair_ref[...].astype(F32).reshape(positions, cz)
        pn = normalize(pair, -1).astype(BF16)
        pn_ref[...] = pn
        bias = dot(bias_w_ref[...], pn, ((1,), (1,)))
        bias = jnp.concatenate([bias[:, :half], bias[:, half:]], axis=0).astype(BF16)
        brecv[pl.ds(col * rows + row, 1)] = bias[None]
        k_of = lane_blocks((1, positions), pair_cols)
        mask = jnp.zeros((1, positions), F32)
        for k in range(pair_rows):
            mask = jnp.where(k_of == k, flags_smem[row * pair_rows + k].astype(F32), mask)
        edge = (
            mask
            * jax.nn.sigmoid(dot(edge_w[0], pn, ((1,), (1,))))
            * dot(edge_w[1], pn, ((1,), (1,)))
        )
        edge = edge.reshape(count, 2 * mine, positions)
        send[...] = jnp.concatenate([edge[:, :, :half], edge[:, :, half:]], axis=1).astype(BF16)

    pl.semaphore_wait(barrier, count - 1)

    for step in range(1, rows):
        pltpu.make_async_remote_copy(
            src_ref=brecv.at[col * rows + row],
            dst_ref=brecv.at[col * rows + row],
            send_sem=r_send_sem,
            recv_sem=r_recv_sem,
            device_id=(lax.rem(row + step, rows), col),
            device_id_type=MESH,
        ).start()

    def push(step, carry):
        to_row, to_col = other(step)
        slot = to_row * cols + to_col
        pltpu.make_async_remote_copy(
            src_ref=send.at[slot],
            dst_ref=recv.at[me],
            send_sem=e_send_sem,
            recv_sem=e_recv_sem,
            device_id=(to_row, to_col),
            device_id_type=MESH,
        ).start()
        return carry

    lax.fori_loop(1, count, push, 0)
    for step in range(1, cols):
        peer = lax.rem(col + step, cols)
        pltpu.make_async_remote_copy(
            src_ref=x_ref.at[pl.ds(peer * seqs, seqs)],
            dst_ref=hx.at[col],
            send_sem=x_send_sem,
            recv_sem=x_recv_sem,
            device_id=(row, peer),
            device_id_type=MESH,
        ).start()
    recv[pl.ds(me, 1)] = send[pl.ds(me, 1)]

    def wait_for(ref, number, sem):
        part = ref.at[pl.ds(0, number)]
        pltpu.make_async_copy(part, part, sem).wait()

    wait_for(brecv, rows - 1, r_recv_sem)
    for step in range(1, cols):
        pltpu.make_async_remote_copy(
            src_ref=brecv.at[pl.ds(col * rows, rows)],
            dst_ref=brecv.at[pl.ds(col * rows, rows)],
            send_sem=c_send_sem,
            recv_sem=c_recv_sem,
            device_id=(row, lax.rem(col + step, cols)),
            device_id_type=MESH,
        ).start()

    own.wait()
    wait_for(hx, cols - 1, x_recv_sem)
    for load in loads[5:]:
        load.wait()
    with jax.named_scope("projections"):
        for c in range(cols):
            shape = (seqs, residues, depth)
            x = hx[c].reshape(seqs * residues, depth).astype(F32)
            xn = normalize(x, -1).astype(BF16)
            queries = dot(xn, wq_ref[...]) * width ** (-0.5)
            q_ref[c] = queries.astype(BF16).reshape(shape)
            kv = dot(xn, wkv_ref[...]).astype(BF16)
            k_ref[c] = kv[:, :depth].reshape(shape)
            v_ref[c] = kv[:, depth:].reshape(shape)
            g_ref[c] = jax.nn.sigmoid(dot(xn, wg_ref[...])).reshape(shape)

    wait_for(recv, count - 1, e_recv_sem)

    block = pair_cols
    lanes = total_res
    per_tile = lanes // block
    where_block = lane_blocks((16 * rows, lanes), block)

    def to_matrices(part, pieces_of):
        for tile in range(half // lanes):
            pieces = pieces_of(tile)
            for k in range(per_tile):
                merged = shift_lanes(pieces[0], (0 - k) * block)
                for c in range(1, cols):
                    merged = jnp.where(
                        where_block == c, shift_lanes(pieces[c], (c - k) * block), merged
                    )
                zed[part, pl.ds(tile * per_tile + k, 16 * rows, stride=8), :] = merged

    def edge_pieces(tile):
        taken = recv[:, :, tile * lanes : (tile + 1) * lanes]
        taken = taken.astype(F32).reshape(rows, cols, 16, lanes)
        return [taken[:, c].reshape(16 * rows, lanes) for c in range(cols)]

    def bias_pieces(tile):
        taken = brecv[:, :, tile * lanes : (tile + 1) * lanes]
        taken = taken.astype(F32).reshape(cols, 16 * rows, lanes)
        return [taken[c] for c in range(cols)]

    with jax.named_scope("edge_matrices"):
        to_matrices(0, edge_pieces)

    def matrix(part, q):
        return zed[part].reshape(2 * rows, 8, 8, lanes)[:, q].reshape(total_res, lanes)

    with jax.named_scope("triangle_product"):
        for ch in range(mine):
            left = matrix(0, ch).T.astype(BF16)
            right = matrix(0, mine + ch).astype(BF16)
            product = dot(left, right).reshape(2 * rows, 8, lanes)
            zprod[:, ch] = product
        where_small = lane_blocks((2 * rows * mine, lanes), block)
        for tile in range(half // lanes):
            taken = [
                zprod.reshape(2 * rows * mine * 8, lanes)[
                    pl.ds(tile * per_tile + k, 2 * rows * mine, stride=8), :
                ]
                for k in range(per_tile)
            ]
            merged_all = []
            for c in range(cols):
                merged = shift_lanes(taken[0], (0 - c) * block)
                for k in range(1, per_tile):
                    merged = jnp.where(
                        where_small == k, shift_lanes(taken[k], (k - c) * block), merged
                    )
                merged_all.append(merged.reshape(rows, 2 * mine, lanes))
            psend[:, :, tile * lanes : (tile + 1) * lanes] = jnp.stack(
                merged_all, axis=1
            ).reshape(count, 2 * mine, lanes)

    def push_product(step, carry):
        to_row, to_col = other(step)
        slot = to_row * cols + to_col
        pltpu.make_async_remote_copy(
            src_ref=psend.at[slot],
            dst_ref=precv.at[me],
            send_sem=p_send_sem,
            recv_sem=p_recv_sem,
            device_id=(to_row, to_col),
            device_id_type=MESH,
        ).start()
        return carry

    lax.fori_loop(1, count, push_product, 0)
    precv[pl.ds(me, 1)] = psend[pl.ds(me, 1)]

    wait_for(brecv, (cols - 1) * rows, c_recv_sem)
    with jax.named_scope("attention_bias"):
        to_matrices(1, bias_pieces)
        identity = jnp.broadcast_to(identity_ref[...].astype(F32), (total_res, total_res))
        cross = (identity.T != identity).astype(F32)
        for h in range(heads):
            extra[h] = matrix(1, h) + offset_ref[h] * cross

    keep = keep_ref[...] > 0
    head_of = lane_blocks((total_res, depth), width)
    in_head = [(lane_blocks((1, depth), width) == h).astype(F32).astype(BF16) for h in range(heads)]
    at_once = 2 if seqs % 2 == 0 else 1

    def attend(s):
        queries = q_ref[:, s].reshape(total_res, depth)
        keys = k_ref[:, s].reshape(total_res, depth)
        values = v_ref[:, s].reshape(total_res, depth)
        key_stack = jnp.concatenate([keys * in_head[h] for h in range(heads)], axis=0)
        value_stack = jnp.concatenate([values * in_head[h] for h in range(heads)], axis=0)
        scores = dot(queries, key_stack, ((1,), (1,)))
        probs = []
        total = jnp.ones((total_res, depth), F32)
        for h in range(heads):
            one = scores[:, h * total_res : (h + 1) * total_res] + extra[h]
            one = jnp.where(keep, one, -1000000000.0)
            one = jnp.exp(one - jnp.max(one, axis=-1, keepdims=True))
            total = jnp.where(head_of == h, jnp.sum(one, axis=-1, keepdims=True), total)
            probs.append(one.astype(BF16))
        attended = dot(jnp.concatenate(probs, axis=1), value_stack) / total
        gate = g_ref[:, s].reshape(total_res, depth)
        gated = (gate * attended).astype(BF16)
        x = hx[:, s].reshape(total_res, depth).astype(F32)
        result = (x + dot(gated, wo_ref[...])).astype(BF16)
        return result.reshape(cols, residues, depth)

    def attend_group(group, carry):
        first = group * at_once
        results = [attend(first + n) for n in range(at_once)]
        for n in range(at_once):
            hout[:, first + n] = results[n]
        for step in range(1, cols):
            peer = lax.rem(col + step, cols)
            pltpu.make_async_remote_copy(
                src_ref=hout.at[peer, pl.ds(first, at_once)],
                dst_ref=msa_out_ref.at[pl.ds(col * seqs + first, at_once)],
                send_sem=o_send_sem,
                recv_sem=o_recv_sem,
                device_id=(row, peer),
                device_id_type=MESH,
            ).start()
        msa_out_ref[pl.ds(col * seqs + first, at_once)] = hout[col, pl.ds(first, at_once)]
        return carry

    with jax.named_scope("row_attention"):
        lax.fori_loop(0, seqs // at_once, attend_group, 0)

    wait_for(precv, count - 1, p_recv_sem)
    loads[3].wait()
    loads[4].wait()
    with jax.named_scope("pair_update"):
        product = precv[...]
        in_half = lax.broadcasted_iota(jnp.int32, (8, half), 0) < mine

        def spread_halves(partial):
            low = jnp.sum(jnp.where(in_half, partial, 0.0), axis=0, keepdims=True)
            high = jnp.sum(jnp.where(in_half, 0.0, partial), axis=0, keepdims=True)
            return jnp.where(in_half, low, high) / channels

        center = product - spread_halves(jnp.sum(product, axis=0))[None]
        spread = spread_halves(jnp.sum(center * center, axis=0))
        norm = (center * lax.rsqrt(spread + 1e-05)[None]).reshape(count * 8, half)
        to = lax.broadcasted_iota(jnp.int32, (2 * channels, channels), 0)
        source = lax.broadcasted_iota(jnp.int32, (2 * channels, channels), 1)
        wanted = to // (2 * mine) * mine + to % mine
        final_w = dot((source == wanted).astype(BF16), tri_out_w_ref[...])
        low_rows = to % (2 * mine) < mine
        final_w = jnp.concatenate(
            [jnp.where(low_rows, final_w, 0.0), jnp.where(low_rows, 0.0, final_w)], axis=1
        ).astype(BF16)
        update = dot(norm.T.astype(BF16), final_w)
        update = jnp.concatenate([update[:, :cz], update[:, cz:]], axis=0)
        tri_gate = jax.nn.sigmoid(dot(pn_ref[...], tri_gate_w_ref[...]))
        pair = pair_ref[...].astype(F32).reshape(positions, cz)
        pair_out_ref[...] = (
            (pair + tri_gate * update).astype(BF16).reshape(pair_rows, pair_cols, cz)
        )

    wait_for(hx, cols - 1, x_send_sem)
    wait_for(send, count - 1, e_send_sem)
    wait_for(psend, count - 1, p_send_sem)
    wait_for(brecv, rows - 1, r_send_sem)
    wait_for(brecv, (cols - 1) * rows, c_send_sem)
    wait_for(hout, cols - 1, o_send_sem)
    wait_for(hout, cols - 1, o_recv_sem)


def local_fused(
    rows,
    cols,
    homolog_tensor,
    pairwise_tensor,
    genuine_amino_flags,
    polymer_identity,
    asking_weights,
    attend_sigmoid_weights,
    lookup_content_weights,
    attend_final_weights,
    pairwise_logit_weights,
    crosspolymer_offset,
    outgoing_link_weights,
    incoming_link_weights,
    trimult_sigmoid_weights,
    trimult_final_weights,
):
    count = rows * cols
    homologs, residues, depth = homolog_tensor.shape
    pair_rows, pair_cols, cz = pairwise_tensor.shape
    heads = pairwise_logit_weights.shape[1]
    total_res = cols * residues
    seqs = homologs // cols
    mine = cz // count
    half = pair_rows * pair_cols // 2
    vmem = pl.BlockSpec(memory_space=pltpu.VMEM)
    smem = pl.BlockSpec(memory_space=pltpu.SMEM)
    hbm = pl.BlockSpec(memory_space=pltpu.HBM)
    dma = pltpu.SemaphoreType.DMA
    msa_block = (cols, seqs, residues, depth)
    return pl.pallas_call(
        functools.partial(fused, (rows, cols, heads, cz)),
        out_shape=(
            jax.ShapeDtypeStruct(homolog_tensor.shape, BF16),
            jax.ShapeDtypeStruct(pairwise_tensor.shape, BF16),
        ),
        in_specs=[hbm, hbm, smem, vmem, vmem, smem] + [hbm] * 4 + [vmem] + [hbm] * 4,
        out_specs=(vmem, vmem),
        scratch_shapes=[
            pltpu.VMEM(msa_block, BF16),
            pltpu.VMEM(msa_block, BF16),
            pltpu.VMEM((count, 16, half), BF16),
            pltpu.VMEM((count, 16, half), BF16),
            pltpu.VMEM((count, 16, half), BF16),
            pltpu.VMEM((count, 2 * mine, half), F32),
            pltpu.VMEM((count, 2 * mine, half), F32),
            pltpu.VMEM((2, 8 * total_res, total_res), F32),
            pltpu.VMEM((2 * rows, mine, 8, total_res), F32),
            pltpu.VMEM((heads, total_res, total_res), F32),
            pltpu.VMEM((pair_rows * pair_cols, cz), BF16),
            pltpu.VMEM(msa_block, BF16),
            pltpu.VMEM(msa_block, BF16),
            pltpu.VMEM(msa_block, BF16),
            pltpu.VMEM(msa_block, F32),
            pltpu.VMEM((pair_rows, pair_cols, cz), BF16),
            pltpu.VMEM(asking_weights.shape, BF16),
            pltpu.VMEM(attend_sigmoid_weights.shape, BF16),
            pltpu.VMEM(lookup_content_weights.shape, BF16),
            pltpu.VMEM(attend_final_weights.shape, BF16),
            pltpu.VMEM(outgoing_link_weights.shape, BF16),
            pltpu.VMEM(incoming_link_weights.shape, BF16),
            pltpu.VMEM(trimult_sigmoid_weights.shape, BF16),
            pltpu.VMEM(trimult_final_weights.shape, BF16),
            dma((9,)),
        ]
        + [dma] * 13,
        compiler_params=pltpu.CompilerParams(
            collective_id=0, has_side_effects=True, vmem_limit_bytes=62 * 2**20
        ),
    )(
        homolog_tensor,
        pairwise_tensor,
        genuine_amino_flags,
        genuine_amino_flags.reshape(1, -1),
        polymer_identity.reshape(1, -1),
        crosspolymer_offset,
        asking_weights,
        attend_sigmoid_weights,
        lookup_content_weights,
        attend_final_weights,
        jnp.transpose(pairwise_logit_weights),
        outgoing_link_weights,
        incoming_link_weights,
        trimult_sigmoid_weights,
        trimult_final_weights,
    )


def from_root(array, axis, root):
    mine = lax.axis_index(axis) == root
    return lax.psum(jnp.where(mine, array, jnp.zeros_like(array)), axis)


def standardize_features(tensor):
    tensor = tensor.astype(jnp.float32)
    center = tensor - jnp.mean(tensor, axis=-1, keepdims=True)
    spread = jnp.mean(center * center, axis=-1, keepdims=True)
    return center * lax.rsqrt(spread + 1e-05)


def edges(pair_norm, weight, mask_rows, width):
    projected = jnp.dot(pair_norm, weight, preferred_element_type=jnp.float32)
    edge_vals = (
        mask_rows * jax.nn.sigmoid(projected[..., :width]) * projected[..., width:]
    ).astype(jnp.bfloat16)
    return jnp.transpose(edge_vals, (2, 0, 1))


def local(
    homolog_tensor,
    pairwise_tensor,
    genuine_amino_flags,
    polymer_identity,
    asking_weights,
    attend_sigmoid_weights,
    lookup_content_weights,
    attend_final_weights,
    pairwise_logit_weights,
    crosspolymer_offset,
    outgoing_link_weights,
    incoming_link_weights,
    trimult_sigmoid_weights,
    trimult_final_weights,
):
    row_count = lax.axis_size("row")
    col_count = lax.axis_size("col")
    row_index = lax.axis_index("row")
    col_index = lax.axis_index("col")
    homolog_entries, amino_positions, feature_depth = homolog_tensor.shape
    res_rows = pairwise_tensor.shape[0]
    pair_width = pairwise_tensor.shape[2]
    row_ratio = row_count // col_count
    head_count = pairwise_logit_weights.shape[1]
    inner_width = asking_weights.shape[1]
    per_head_width = inner_width // head_count
    standardized_homologs = standardize_features(homolog_tensor).astype(jnp.bfloat16)
    pair_norm = standardize_features(pairwise_tensor).astype(jnp.bfloat16)
    local_bias = jnp.einsum(
        "ijc,ch->hij", pair_norm, pairwise_logit_weights, preferred_element_type=jnp.float32
    ).astype(jnp.bfloat16)
    row_bias = lax.all_gather(local_bias, "col", axis=2, tiled=True)
    queries = (
        jnp.dot(standardized_homologs, asking_weights, preferred_element_type=jnp.float32)
        * per_head_width ** (-0.5)
    ).astype(jnp.bfloat16)
    queries = queries.reshape(homolog_entries, amino_positions, head_count, per_head_width)
    gate_activation = jax.nn.sigmoid(
        jnp.dot(standardized_homologs, attend_sigmoid_weights, preferred_element_type=jnp.float32)
    )
    all_bias = lax.all_gather(row_bias, "row", axis=1, tiled=True)
    bias_block = lax.dynamic_slice_in_dim(all_bias, col_index * amino_positions, amino_positions, 1)
    query_chain = lax.dynamic_slice_in_dim(
        polymer_identity, col_index * amino_positions, amino_positions, 0
    )
    cross_chain = (query_chain[:, None] != polymer_identity[None, :]).astype(jnp.float32)
    extra_bias = (
        bias_block.astype(jnp.float32) + crosspolymer_offset[:, None, None] * cross_chain[None]
    )
    keep_all = genuine_amino_flags > 0
    key_value = jnp.dot(
        lax.all_gather(standardized_homologs, "col", axis=1, tiled=True),
        lookup_content_weights,
        preferred_element_type=jnp.float32,
    ).astype(jnp.bfloat16)
    piece_len = key_value.shape[1]
    key_rows = key_value[..., :inner_width].reshape(
        homolog_entries, piece_len, head_count, per_head_width
    )
    value_rows = key_value[..., inner_width:].reshape(
        homolog_entries, piece_len, head_count, per_head_width
    )
    scores = jnp.einsum("sqhd,skhd->shqk", queries, key_rows, preferred_element_type=jnp.float32)
    scores = scores + extra_bias[None]
    scores = jnp.where(keep_all, scores, -1000000000.0)
    peak_old = jnp.full((homolog_entries, head_count, amino_positions), -jnp.inf, jnp.float32)
    total_old = jnp.zeros((homolog_entries, head_count, amino_positions), jnp.float32)
    accum_old = jnp.zeros(
        (homolog_entries, head_count, amino_positions, per_head_width), jnp.float32
    )
    peak_now = jnp.max(scores, axis=-1)
    factor = jnp.exp(peak_old - peak_now)
    exp_scores = jnp.exp(scores - peak_now[..., None])
    total_now = total_old * factor + jnp.sum(exp_scores, axis=-1)
    accum_now = accum_old * factor[..., None] + jnp.einsum(
        "shqk,skhd->shqd",
        exp_scores.astype(jnp.bfloat16),
        value_rows,
        preferred_element_type=jnp.float32,
    )
    peak_now, total_now, accum_now = (peak_now, total_now, accum_now)
    attended = accum_now / total_now[..., None]
    attended = jnp.transpose(attended, (0, 2, 1, 3)).reshape(
        homolog_entries, amino_positions, inner_width
    )
    gated_output = (gate_activation * attended).astype(jnp.bfloat16)
    attended_homologs = (
        homolog_tensor.astype(jnp.float32)
        + jnp.dot(gated_output, attend_final_weights, preferred_element_type=jnp.float32)
    ).astype(jnp.bfloat16)
    mask_rows = lax.dynamic_slice_in_dim(
        genuine_amino_flags, row_index * res_rows, res_rows, 0
    ).astype(jnp.float32)[:, None, None]
    left_tri = edges(pair_norm, outgoing_link_weights, mask_rows, pair_width)
    right_tri = edges(pair_norm, incoming_link_weights, mask_rows, pair_width)
    left_cols = lax.all_gather(left_tri, "row", axis=1, tiled=True)
    left_part = lax.dynamic_slice_in_dim(left_cols, row_index % row_ratio * res_rows, res_rows, 2)
    left_mine = from_root(left_part, "col", row_index // row_ratio)
    product = jnp.einsum(
        "cki,ckj->cij",
        left_mine,
        lax.all_gather(right_tri, "row", axis=1, tiled=True),
        preferred_element_type=jnp.float32,
    )
    product_norm = standardize_features(jnp.transpose(product, (1, 2, 0))).astype(jnp.bfloat16)
    tri_gate = jax.nn.sigmoid(
        jnp.dot(pair_norm, trimult_sigmoid_weights, preferred_element_type=jnp.float32)
    )
    update = jnp.dot(product_norm, trimult_final_weights, preferred_element_type=jnp.float32)
    pair_output = (pairwise_tensor.astype(jnp.float32) + tri_gate * update).astype(jnp.bfloat16)
    return (attended_homologs, pair_output)


def solution(mesh):
    in_specs = (
        P("row", "col", None),
        P("row", "col", None),
        P(),
        P(),
        P(),
        P(),
        P(),
        P(),
        P(),
        P(),
        P(),
        P(),
        P(),
        P(),
    )
    out_specs = (P("row", "col", None), P("row", "col", None))

    def local_either(*blocks):
        rows, cols = mesh.shape["row"], mesh.shape["col"]
        homologs, residues, depth = blocks[0].shape
        pair_rows, pair_cols, cz = blocks[1].shape
        heads = blocks[8].shape[1]
        fits = (
            cz == 4 * rows * cols
            and cz == cols * residues
            and cz == rows * pair_rows
            and pair_cols == residues == 32
            and pair_rows == 16
            and heads == 8
            and homologs % cols == 0
            and blocks[4].shape[1] == depth
            and depth % 128 == 0
        )
        if fits:
            return local_fused(rows, cols, *blocks)
        return local(*blocks)

    return jax.shard_map(local_either, mesh=mesh, in_specs=in_specs, out_specs=out_specs, check_vma=False)
```

```python
import functools

import jax
import jax.numpy as jnp
from jax import lax
from jax.experimental import pallas as pl
from jax.experimental.pallas import tpu as pltpu
from jax.sharding import PartitionSpec as P

MESH = pl.DeviceIdType.MESH
F32 = jnp.float32
BF16 = jnp.bfloat16


def dot(a, b, contract=((1,), (0,))):
    return lax.dot_general(a, b, (contract, ((), ())), preferred_element_type=F32)


def normalize(x, axis):
    center = x - jnp.mean(x, axis=axis, keepdims=True)
    spread = jnp.mean(center * center, axis=axis, keepdims=True)
    return center * lax.rsqrt(spread + 1e-05)


def lane_blocks(shape, width):
    return lax.broadcasted_iota(jnp.int32, shape, len(shape) - 1) // width


def shift_lanes(x, amount):
    amount = amount % x.shape[-1]
    return x if amount == 0 else pltpu.roll(x, amount, x.ndim - 1)


def fused(
    dims,
    x_ref,
    pair_hbm,
    flags_smem,
    keep_ref,
    identity_ref,
    offset_ref,
    wq_hbm,
    wg_hbm,
    wkv_hbm,
    wo_hbm,
    bias_w_ref,
    left_w_hbm,
    right_w_hbm,
    tri_gate_w_hbm,
    tri_out_w_hbm,
    msa_out_ref,
    pair_out_ref,
    hx,
    hout,
    send,
    recv,
    brecv,
    psend,
    precv,
    zed,
    zprod,
    extra,
    pn_ref,
    q_ref,
    k_ref,
    v_ref,
    g_ref,
    pair_ref,
    wq_ref,
    wg_ref,
    wkv_ref,
    wo_ref,
    left_w_ref,
    right_w_ref,
    tri_gate_w_ref,
    tri_out_w_ref,
    in_sem,
    own_sem,
    x_send_sem,
    x_recv_sem,
    e_send_sem,
    e_recv_sem,
    p_send_sem,
    p_recv_sem,
    o_send_sem,
    o_recv_sem,
    r_send_sem,
    r_recv_sem,
    c_send_sem,
    c_recv_sem,
):
    rows, cols, heads, channels = dims
    count = rows * cols
    mine = channels // count
    row = lax.axis_index("row")
    col = lax.axis_index("col")
    me = row * cols + col
    seqs, residues, depth = hx.shape[1:]
    total_res = cols * residues
    width = depth // heads
    pair_rows, pair_cols, cz = pair_ref.shape
    positions = pair_rows * pair_cols
    half = positions // 2
    both = 2 * cz

    def other(step):
        peer = lax.rem(me + step, count)
        return peer // cols, lax.rem(peer, cols)

    barrier = pltpu.get_barrier_semaphore()

    def greet(step, carry):
        pl.semaphore_signal(barrier, inc=1, device_id=other(step), device_id_type=MESH)
        return carry

    loads = [
        pltpu.make_async_copy(source, target, in_sem.at[n])
        for n, (source, target) in enumerate(
            (
                (pair_hbm, pair_ref),
                (left_w_hbm, left_w_ref),
                (right_w_hbm, right_w_ref),
                (tri_out_w_hbm, tri_out_w_ref),
                (tri_gate_w_hbm, tri_gate_w_ref),
                (wq_hbm, wq_ref),
                (wkv_hbm, wkv_ref),
                (wg_hbm, wg_ref),
                (wo_hbm, wo_ref),
            )
        )
    ]
    for load in loads:
        load.start()
    own = pltpu.make_async_copy(x_ref.at[pl.ds(col * seqs, seqs)], hx.at[col], own_sem)
    own.start()
    lax.fori_loop(1, count, greet, 0)

    with jax.named_scope("weights_by_owner"):
        to = lax.broadcasted_iota(jnp.int32, (both, both), 0)
        source = lax.broadcasted_iota(jnp.int32, (both, both), 1)
        wanted = (to % (2 * mine)) // mine * cz + to // (2 * mine) * mine + to % mine
        order = (source == wanted).astype(BF16)
        loads[1].wait()
        loads[2].wait()
        edge_w = [
            dot(
                order,
                jnp.concatenate(
                    [left_w_ref[:, n * cz : n * cz + cz], right_w_ref[:, n * cz : n * cz + cz]],
                    axis=1,
                ),
                ((1,), (1,)),
            ).astype(BF16)
            for n in range(2)
        ]

    pl.semaphore_wait(barrier, count - 1)
    for step in range(1, cols):
        peer = lax.rem(col + step, cols)
        pltpu.make_async_remote_copy(
            src_ref=x_ref.at[pl.ds(peer * seqs, seqs)],
            dst_ref=hx.at[col],
            send_sem=x_send_sem,
            recv_sem=x_recv_sem,
            device_id=(row, peer),
            device_id_type=MESH,
        ).start()

    with jax.named_scope("pair_bias"):
        loads[0].wait()
        pair = pair_ref[...].astype(F32).reshape(positions, cz)
        pn = normalize(pair, -1).astype(BF16)
        pn_ref[...] = pn
        bias = dot(bias_w_ref[...], pn, ((1,), (1,)))
        bias = jnp.concatenate([bias[:, :half], bias[:, half:]], axis=0).astype(BF16)
        brecv[pl.ds(col * rows + row, 1)] = bias[None]

    for step in range(1, rows):
        pltpu.make_async_remote_copy(
            src_ref=brecv.at[col * rows + row],
            dst_ref=brecv.at[col * rows + row],
            send_sem=r_send_sem,
            recv_sem=r_recv_sem,
            device_id=(lax.rem(row + step, rows), col),
            device_id_type=MESH,
        ).start()

    with jax.named_scope("pair_edges"):
        k_of = lane_blocks((1, positions), pair_cols)
        mask = jnp.zeros((1, positions), F32)
        for k in range(pair_rows):
            mask = jnp.where(k_of == k, flags_smem[row * pair_rows + k].astype(F32), mask)
        edge = (
            mask
            * jax.nn.sigmoid(dot(edge_w[0], pn, ((1,), (1,))))
            * dot(edge_w[1], pn, ((1,), (1,)))
        )
        edge = edge.reshape(count, 2 * mine, positions)
        send[...] = jnp.concatenate([edge[:, :, :half], edge[:, :, half:]], axis=1).astype(BF16)

    recv[pl.ds(me, 1)] = send[pl.ds(me, 1)]

    def wait_for(ref, number, sem):
        part = ref.at[pl.ds(0, number)]
        pltpu.make_async_copy(part, part, sem).wait()

    wait_for(brecv, rows - 1, r_recv_sem)
    for step in range(1, cols):
        pltpu.make_async_remote_copy(
            src_ref=brecv.at[pl.ds(col * rows, rows)],
            dst_ref=brecv.at[pl.ds(col * rows, rows)],
            send_sem=c_send_sem,
            recv_sem=c_recv_sem,
            device_id=(row, lax.rem(col + step, cols)),
            device_id_type=MESH,
        ).start()

    def push(step, carry):
        to_row, to_col = other(step)
        slot = to_row * cols + to_col
        pltpu.make_async_remote_copy(
            src_ref=send.at[slot],
            dst_ref=recv.at[me],
            send_sem=e_send_sem,
            recv_sem=e_recv_sem,
            device_id=(to_row, to_col),
            device_id_type=MESH,
        ).start()
        return carry

    lax.fori_loop(1, count, push, 0)
    own.wait()
    wait_for(hx, cols - 1, x_recv_sem)
    for load in loads[5:]:
        load.wait()
    with jax.named_scope("projections"):
        for c in range(cols):
            shape = (seqs, residues, depth)
            x = hx[c].reshape(seqs * residues, depth).astype(F32)
            xn = normalize(x, -1).astype(BF16)
            queries = dot(xn, wq_ref[...]) * width ** (-0.5)
            q_ref[c] = queries.astype(BF16).reshape(shape)
            kv = dot(xn, wkv_ref[...]).astype(BF16)
            k_ref[c] = kv[:, :depth].reshape(shape)
            v_ref[c] = kv[:, depth:].reshape(shape)
            g_ref[c] = jax.nn.sigmoid(dot(xn, wg_ref[...])).reshape(shape)

    block = pair_cols
    lanes = total_res
    per_tile = lanes // block
    where_block = lane_blocks((16 * rows, lanes), block)

    def to_matrices(part, pieces_of):
        for tile in range(half // lanes):
            pieces = pieces_of(tile)
            for k in range(per_tile):
                merged = shift_lanes(pieces[0], (0 - k) * block)
                for c in range(1, cols):
                    merged = jnp.where(
                        where_block == c, shift_lanes(pieces[c], (c - k) * block), merged
                    )
                zed[part, pl.ds(tile * per_tile + k, 16 * rows, stride=8), :] = merged

    def edge_pieces(tile):
        taken = recv[:, :, tile * lanes : (tile + 1) * lanes]
        taken = taken.astype(F32).reshape(rows, cols, 16, lanes)
        return [taken[:, c].reshape(16 * rows, lanes) for c in range(cols)]

    def bias_pieces(tile):
        taken = brecv[:, :, tile * lanes : (tile + 1) * lanes]
        taken = taken.astype(F32).reshape(cols, 16 * rows, lanes)
        return [taken[c] for c in range(cols)]

    def matrix(part, q):
        return zed[part].reshape(2 * rows, 8, 8, lanes)[:, q].reshape(total_res, lanes)

    wait_for(brecv, (cols - 1) * rows, c_recv_sem)
    with jax.named_scope("attention_bias"):
        to_matrices(1, bias_pieces)
        identity = jnp.broadcast_to(identity_ref[...].astype(F32), (total_res, total_res))
        cross = (identity.T != identity).astype(F32)
        for h in range(heads):
            extra[h] = matrix(1, h) + offset_ref[h] * cross

    keep = keep_ref[...] > 0
    head_of = lane_blocks((total_res, 128), width)
    in_head = [(lane_blocks((1, depth), width) == h).astype(F32).astype(BF16) for h in range(heads)]
    at_once = 2 if seqs % 2 == 0 else 1

    def attend(s):
        queries = q_ref[:, s].reshape(total_res, depth)
        keys = k_ref[:, s].reshape(total_res, depth)
        values = v_ref[:, s].reshape(total_res, depth)
        key_stack = jnp.concatenate([keys * in_head[h] for h in range(heads)], axis=0)
        value_stack = jnp.concatenate([values * in_head[h] for h in range(heads)], axis=0)
        scores = dot(queries, key_stack, ((1,), (1,)))
        probs = []
        totals = [jnp.ones((total_res, 128), F32)] * (depth // 128)
        in_tile = 128 // width
        for h in range(heads):
            one = scores[:, h * total_res : (h + 1) * total_res] + extra[h]
            one = jnp.where(keep, one, -1000000000.0)
            one = jnp.exp(one - jnp.max(one, axis=-1, keepdims=True))
            totals[h // in_tile] = jnp.where(
                head_of == h % in_tile, jnp.sum(one, axis=-1, keepdims=True), totals[h // in_tile]
            )
            probs.append(one.astype(BF16))
        attended = dot(jnp.concatenate(probs, axis=1), value_stack)
        attended = attended / jnp.concatenate(totals, axis=1)
        gate = g_ref[:, s].reshape(total_res, depth)
        gated = (gate * attended).astype(BF16)
        x = hx[:, s].reshape(total_res, depth).astype(F32)
        result = (x + dot(gated, wo_ref[...])).astype(BF16)
        return result.reshape(cols, residues, depth)

    def attend_group(group, carry):
        first = group * at_once
        results = [attend(first + n) for n in range(at_once)]
        for n in range(at_once):
            hout[:, first + n] = results[n]
        for step in range(1, cols):
            peer = lax.rem(col + step, cols)
            pltpu.make_async_remote_copy(
                src_ref=hout.at[peer, pl.ds(first, at_once)],
                dst_ref=msa_out_ref.at[pl.ds(col * seqs + first, at_once)],
                send_sem=o_send_sem,
                recv_sem=o_recv_sem,
                device_id=(row, peer),
                device_id_type=MESH,
            ).start()
        msa_out_ref[pl.ds(col * seqs + first, at_once)] = hout[col, pl.ds(first, at_once)]
        return carry

    with jax.named_scope("row_attention"):
        lax.fori_loop(0, seqs // at_once // 2, attend_group, 0)

    wait_for(recv, count - 1, e_recv_sem)
    with jax.named_scope("edge_matrices"):
        to_matrices(0, edge_pieces)
    with jax.named_scope("triangle_product"):
        for ch in range(mine):
            left = matrix(0, ch).T.astype(BF16)
            right = matrix(0, mine + ch).astype(BF16)
            product = dot(left, right).reshape(2 * rows, 8, lanes)
            zprod[:, ch] = product
        where_small = lane_blocks((2 * rows * mine, lanes), block)
        for tile in range(half // lanes):
            taken = [
                zprod.reshape(2 * rows * mine * 8, lanes)[
                    pl.ds(tile * per_tile + k, 2 * rows * mine, stride=8), :
                ]
                for k in range(per_tile)
            ]
            merged_all = []
            for c in range(cols):
                merged = shift_lanes(taken[0], (0 - c) * block)
                for k in range(1, per_tile):
                    merged = jnp.where(
                        where_small == k, shift_lanes(taken[k], (k - c) * block), merged
                    )
                merged_all.append(merged.reshape(rows, 2 * mine, lanes))
            psend[:, :, tile * lanes : (tile + 1) * lanes] = jnp.stack(
                merged_all, axis=1
            ).reshape(count, 2 * mine, lanes)

    def push_product(step, carry):
        to_row, to_col = other(step)
        slot = to_row * cols + to_col
        pltpu.make_async_remote_copy(
            src_ref=psend.at[slot],
            dst_ref=precv.at[me],
            send_sem=p_send_sem,
            recv_sem=p_recv_sem,
            device_id=(to_row, to_col),
            device_id_type=MESH,
        ).start()
        return carry

    lax.fori_loop(1, count, push_product, 0)
    precv[pl.ds(me, 1)] = psend[pl.ds(me, 1)]

    with jax.named_scope("row_attention"):
        lax.fori_loop(seqs // at_once // 2, seqs // at_once, attend_group, 0)

    wait_for(precv, count - 1, p_recv_sem)
    loads[3].wait()
    loads[4].wait()
    with jax.named_scope("pair_update"):
        product = precv[...]
        in_half = lax.broadcasted_iota(jnp.int32, (8, half), 0) < mine

        def spread_halves(partial):
            low = jnp.sum(jnp.where(in_half, partial, 0.0), axis=0, keepdims=True)
            high = jnp.sum(jnp.where(in_half, 0.0, partial), axis=0, keepdims=True)
            return jnp.where(in_half, low, high) / channels

        center = product - spread_halves(jnp.sum(product, axis=0))[None]
        spread = spread_halves(jnp.sum(center * center, axis=0))
        norm = (center * lax.rsqrt(spread + 1e-05)[None]).reshape(count * 8, half)
        to = lax.broadcasted_iota(jnp.int32, (2 * channels, channels), 0)
        source = lax.broadcasted_iota(jnp.int32, (2 * channels, channels), 1)
        wanted = to // (2 * mine) * mine + to % mine
        final_w = dot((source == wanted).astype(BF16), tri_out_w_ref[...])
        low_rows = to % (2 * mine) < mine
        final_w = jnp.concatenate(
            [jnp.where(low_rows, final_w, 0.0), jnp.where(low_rows, 0.0, final_w)], axis=1
        ).astype(BF16)
        update = dot(norm.T.astype(BF16), final_w)
        update = jnp.concatenate([update[:, :cz], update[:, cz:]], axis=0)
        tri_gate = jax.nn.sigmoid(dot(pn_ref[...], tri_gate_w_ref[...]))
        pair = pair_ref[...].astype(F32).reshape(positions, cz)
        pair_out_ref[...] = (
            (pair + tri_gate * update).astype(BF16).reshape(pair_rows, pair_cols, cz)
        )

    wait_for(hx, cols - 1, x_send_sem)
    wait_for(send, count - 1, e_send_sem)
    wait_for(psend, count - 1, p_send_sem)
    wait_for(brecv, rows - 1, r_send_sem)
    wait_for(brecv, (cols - 1) * rows, c_send_sem)
    wait_for(hout, cols - 1, o_send_sem)
    wait_for(hout, cols - 1, o_recv_sem)


def local_fused(
    rows,
    cols,
    homolog_tensor,
    pairwise_tensor,
    genuine_amino_flags,
    polymer_identity,
    asking_weights,
    attend_sigmoid_weights,
    lookup_content_weights,
    attend_final_weights,
    pairwise_logit_weights,
    crosspolymer_offset,
    outgoing_link_weights,
    incoming_link_weights,
    trimult_sigmoid_weights,
    trimult_final_weights,
):
    count = rows * cols
    homologs, residues, depth = homolog_tensor.shape
    pair_rows, pair_cols, cz = pairwise_tensor.shape
    heads = pairwise_logit_weights.shape[1]
    total_res = cols * residues
    seqs = homologs // cols
    mine = cz // count
    half = pair_rows * pair_cols // 2
    vmem = pl.BlockSpec(memory_space=pltpu.VMEM)
    smem = pl.BlockSpec(memory_space=pltpu.SMEM)
    hbm = pl.BlockSpec(memory_space=pltpu.HBM)
    dma = pltpu.SemaphoreType.DMA
    msa_block = (cols, seqs, residues, depth)
    return pl.pallas_call(
        functools.partial(fused, (rows, cols, heads, cz)),
        out_shape=(
            jax.ShapeDtypeStruct(homolog_tensor.shape, BF16),
            jax.ShapeDtypeStruct(pairwise_tensor.shape, BF16),
        ),
        in_specs=[hbm, hbm, smem, vmem, vmem, smem] + [hbm] * 4 + [vmem] + [hbm] * 4,
        out_specs=(vmem, vmem),
        scratch_shapes=[
            pltpu.VMEM(msa_block, BF16),
            pltpu.VMEM(msa_block, BF16),
            pltpu.VMEM((count, 16, half), BF16),
            pltpu.VMEM((count, 16, half), BF16),
            pltpu.VMEM((count, 16, half), BF16),
            pltpu.VMEM((count, 2 * mine, half), F32),
            pltpu.VMEM((count, 2 * mine, half), F32),
            pltpu.VMEM((2, 8 * total_res, total_res), F32),
            pltpu.VMEM((2 * rows, mine, 8, total_res), F32),
            pltpu.VMEM((heads, total_res, total_res), F32),
            pltpu.VMEM((pair_rows * pair_cols, cz), BF16),
            pltpu.VMEM(msa_block, BF16),
            pltpu.VMEM(msa_block, BF16),
            pltpu.VMEM(msa_block, BF16),
            pltpu.VMEM(msa_block, F32),
            pltpu.VMEM((pair_rows, pair_cols, cz), BF16),
            pltpu.VMEM(asking_weights.shape, BF16),
            pltpu.VMEM(attend_sigmoid_weights.shape, BF16),
            pltpu.VMEM(lookup_content_weights.shape, BF16),
            pltpu.VMEM(attend_final_weights.shape, BF16),
            pltpu.VMEM(outgoing_link_weights.shape, BF16),
            pltpu.VMEM(incoming_link_weights.shape, BF16),
            pltpu.VMEM(trimult_sigmoid_weights.shape, BF16),
            pltpu.VMEM(trimult_final_weights.shape, BF16),
            dma((9,)),
        ]
        + [dma] * 13,
        compiler_params=pltpu.CompilerParams(
            collective_id=0, has_side_effects=True, vmem_limit_bytes=62 * 2**20
        ),
    )(
        homolog_tensor,
        pairwise_tensor,
        genuine_amino_flags,
        genuine_amino_flags.reshape(1, -1),
        polymer_identity.reshape(1, -1),
        crosspolymer_offset,
        asking_weights,
        attend_sigmoid_weights,
        lookup_content_weights,
        attend_final_weights,
        jnp.transpose(pairwise_logit_weights),
        outgoing_link_weights,
        incoming_link_weights,
        trimult_sigmoid_weights,
        trimult_final_weights,
    )


def from_root(array, axis, root):
    mine = lax.axis_index(axis) == root
    return lax.psum(jnp.where(mine, array, jnp.zeros_like(array)), axis)


def standardize_features(tensor):
    tensor = tensor.astype(jnp.float32)
    center = tensor - jnp.mean(tensor, axis=-1, keepdims=True)
    spread = jnp.mean(center * center, axis=-1, keepdims=True)
    return center * lax.rsqrt(spread + 1e-05)


def edges(pair_norm, weight, mask_rows, width):
    projected = jnp.dot(pair_norm, weight, preferred_element_type=jnp.float32)
    edge_vals = (
        mask_rows * jax.nn.sigmoid(projected[..., :width]) * projected[..., width:]
    ).astype(jnp.bfloat16)
    return jnp.transpose(edge_vals, (2, 0, 1))


def local(
    homolog_tensor,
    pairwise_tensor,
    genuine_amino_flags,
    polymer_identity,
    asking_weights,
    attend_sigmoid_weights,
    lookup_content_weights,
    attend_final_weights,
    pairwise_logit_weights,
    crosspolymer_offset,
    outgoing_link_weights,
    incoming_link_weights,
    trimult_sigmoid_weights,
    trimult_final_weights,
):
    row_count = lax.axis_size("row")
    col_count = lax.axis_size("col")
    row_index = lax.axis_index("row")
    col_index = lax.axis_index("col")
    homolog_entries, amino_positions, feature_depth = homolog_tensor.shape
    res_rows = pairwise_tensor.shape[0]
    pair_width = pairwise_tensor.shape[2]
    row_ratio = row_count // col_count
    head_count = pairwise_logit_weights.shape[1]
    inner_width = asking_weights.shape[1]
    per_head_width = inner_width // head_count
    standardized_homologs = standardize_features(homolog_tensor).astype(jnp.bfloat16)
    pair_norm = standardize_features(pairwise_tensor).astype(jnp.bfloat16)
    local_bias = jnp.einsum(
        "ijc,ch->hij", pair_norm, pairwise_logit_weights, preferred_element_type=jnp.float32
    ).astype(jnp.bfloat16)
    row_bias = lax.all_gather(local_bias, "col", axis=2, tiled=True)
    queries = (
        jnp.dot(standardized_homologs, asking_weights, preferred_element_type=jnp.float32)
        * per_head_width ** (-0.5)
    ).astype(jnp.bfloat16)
    queries = queries.reshape(homolog_entries, amino_positions, head_count, per_head_width)
    gate_activation = jax.nn.sigmoid(
        jnp.dot(standardized_homologs, attend_sigmoid_weights, preferred_element_type=jnp.float32)
    )
    all_bias = lax.all_gather(row_bias, "row", axis=1, tiled=True)
    bias_block = lax.dynamic_slice_in_dim(all_bias, col_index * amino_positions, amino_positions, 1)
    query_chain = lax.dynamic_slice_in_dim(
        polymer_identity, col_index * amino_positions, amino_positions, 0
    )
    cross_chain = (query_chain[:, None] != polymer_identity[None, :]).astype(jnp.float32)
    extra_bias = (
        bias_block.astype(jnp.float32) + crosspolymer_offset[:, None, None] * cross_chain[None]
    )
    keep_all = genuine_amino_flags > 0
    key_value = jnp.dot(
        lax.all_gather(standardized_homologs, "col", axis=1, tiled=True),
        lookup_content_weights,
        preferred_element_type=jnp.float32,
    ).astype(jnp.bfloat16)
    piece_len = key_value.shape[1]
    key_rows = key_value[..., :inner_width].reshape(
        homolog_entries, piece_len, head_count, per_head_width
    )
    value_rows = key_value[..., inner_width:].reshape(
        homolog_entries, piece_len, head_count, per_head_width
    )
    scores = jnp.einsum("sqhd,skhd->shqk", queries, key_rows, preferred_element_type=jnp.float32)
    scores = scores + extra_bias[None]
    scores = jnp.where(keep_all, scores, -1000000000.0)
    peak_old = jnp.full((homolog_entries, head_count, amino_positions), -jnp.inf, jnp.float32)
    total_old = jnp.zeros((homolog_entries, head_count, amino_positions), jnp.float32)
    accum_old = jnp.zeros(
        (homolog_entries, head_count, amino_positions, per_head_width), jnp.float32
    )
    peak_now = jnp.max(scores, axis=-1)
    factor = jnp.exp(peak_old - peak_now)
    exp_scores = jnp.exp(scores - peak_now[..., None])
    total_now = total_old * factor + jnp.sum(exp_scores, axis=-1)
    accum_now = accum_old * factor[..., None] + jnp.einsum(
        "shqk,skhd->shqd",
        exp_scores.astype(jnp.bfloat16),
        value_rows,
        preferred_element_type=jnp.float32,
    )
    peak_now, total_now, accum_now = (peak_now, total_now, accum_now)
    attended = accum_now / total_now[..., None]
    attended = jnp.transpose(attended, (0, 2, 1, 3)).reshape(
        homolog_entries, amino_positions, inner_width
    )
    gated_output = (gate_activation * attended).astype(jnp.bfloat16)
    attended_homologs = (
        homolog_tensor.astype(jnp.float32)
        + jnp.dot(gated_output, attend_final_weights, preferred_element_type=jnp.float32)
    ).astype(jnp.bfloat16)
    mask_rows = lax.dynamic_slice_in_dim(
        genuine_amino_flags, row_index * res_rows, res_rows, 0
    ).astype(jnp.float32)[:, None, None]
    left_tri = edges(pair_norm, outgoing_link_weights, mask_rows, pair_width)
    right_tri = edges(pair_norm, incoming_link_weights, mask_rows, pair_width)
    left_cols = lax.all_gather(left_tri, "row", axis=1, tiled=True)
    left_part = lax.dynamic_slice_in_dim(left_cols, row_index % row_ratio * res_rows, res_rows, 2)
    left_mine = from_root(left_part, "col", row_index // row_ratio)
    product = jnp.einsum(
        "cki,ckj->cij",
        left_mine,
        lax.all_gather(right_tri, "row", axis=1, tiled=True),
        preferred_element_type=jnp.float32,
    )
    product_norm = standardize_features(jnp.transpose(product, (1, 2, 0))).astype(jnp.bfloat16)
    tri_gate = jax.nn.sigmoid(
        jnp.dot(pair_norm, trimult_sigmoid_weights, preferred_element_type=jnp.float32)
    )
    update = jnp.dot(product_norm, trimult_final_weights, preferred_element_type=jnp.float32)
    pair_output = (pairwise_tensor.astype(jnp.float32) + tri_gate * update).astype(jnp.bfloat16)
    return (attended_homologs, pair_output)


def solution(mesh):
    in_specs = (
        P("row", "col", None),
        P("row", "col", None),
        P(),
        P(),
        P(),
        P(),
        P(),
        P(),
        P(),
        P(),
        P(),
        P(),
        P(),
        P(),
    )
    out_specs = (P("row", "col", None), P("row", "col", None))

    def local_either(*blocks):
        rows, cols = mesh.shape["row"], mesh.shape["col"]
        homologs, residues, depth = blocks[0].shape
        pair_rows, pair_cols, cz = blocks[1].shape
        heads = blocks[8].shape[1]
        fits = (
            cz == 4 * rows * cols
            and cz == cols * residues
            and cz == rows * pair_rows
            and pair_cols == residues == 32
            and pair_rows == 16
            and heads == 8
            and homologs % cols == 0
            and blocks[4].shape[1] == depth
            and depth % 128 == 0
        )
        if fits:
            return local_fused(rows, cols, *blocks)
        return local(*blocks)

    return jax.shard_map(local_either, mesh=mesh, in_specs=in_specs, out_specs=out_specs, check_vma=False)
```

```python
import functools

import jax
import jax.numpy as jnp
from jax import lax
from jax.experimental import pallas as pl
from jax.experimental.pallas import tpu as pltpu
from jax.sharding import PartitionSpec as P

MESH = pl.DeviceIdType.MESH
F32 = jnp.float32
BF16 = jnp.bfloat16


def dot(a, b, contract=((1,), (0,))):
    return lax.dot_general(a, b, (contract, ((), ())), preferred_element_type=F32)


def normalize(x, axis):
    center = x - jnp.mean(x, axis=axis, keepdims=True)
    spread = jnp.mean(center * center, axis=axis, keepdims=True)
    return center * lax.rsqrt(spread + 1e-05)


def lane_blocks(shape, width):
    return lax.broadcasted_iota(jnp.int32, shape, len(shape) - 1) // width


def shift_lanes(x, amount):
    amount = amount % x.shape[-1]
    return x if amount == 0 else pltpu.roll(x, amount, x.ndim - 1)


def fused(
    dims,
    x_ref,
    pair_hbm,
    flags_smem,
    keep_ref,
    identity_ref,
    offset_ref,
    wq_hbm,
    wg_hbm,
    wkv_hbm,
    wo_hbm,
    bias_w_ref,
    left_w_hbm,
    right_w_hbm,
    tri_gate_w_hbm,
    tri_out_w_hbm,
    msa_out_ref,
    pair_out_ref,
    hx,
    hout,
    send,
    recv,
    brecv,
    psend,
    precv,
    zed,
    zprod,
    extra,
    pn_ref,
    q_ref,
    k_ref,
    v_ref,
    g_ref,
    key_blocks,
    value_blocks,
    pair_ref,
    wq_ref,
    wg_ref,
    wkv_ref,
    wo_ref,
    left_w_ref,
    right_w_ref,
    tri_gate_w_ref,
    tri_out_w_ref,
    in_sem,
    own_sem,
    x_send_sem,
    x_recv_sem,
    e_send_sem,
    e_recv_sem,
    p_send_sem,
    p_recv_sem,
    o_send_sem,
    o_recv_sem,
    r_send_sem,
    r_recv_sem,
    c_send_sem,
    c_recv_sem,
    keep_sem,
):
    rows, cols, heads, channels = dims
    count = rows * cols
    mine = channels // count
    row = lax.axis_index("row")
    col = lax.axis_index("col")
    me = row * cols + col
    seqs, residues, depth = hx.shape[1:]
    total_res = cols * residues
    width = depth // heads
    pair_rows, pair_cols, cz = pair_ref.shape
    positions = pair_rows * pair_cols
    half = positions // 2
    at_once = key_blocks.shape[0]
    both = 2 * cz

    def other(step):
        peer = lax.rem(me + step, count)
        return peer // cols, lax.rem(peer, cols)

    barrier = pltpu.get_barrier_semaphore()

    def greet(step, carry):
        pl.semaphore_signal(barrier, inc=1, device_id=other(step), device_id_type=MESH)
        return carry

    loads = [
        pltpu.make_async_copy(source, target, in_sem.at[n])
        for n, (source, target) in enumerate(
            (
                (pair_hbm, pair_ref),
                (left_w_hbm, left_w_ref),
                (right_w_hbm, right_w_ref),
                (tri_out_w_hbm, tri_out_w_ref),
                (tri_gate_w_hbm, tri_gate_w_ref),
                (wq_hbm, wq_ref),
                (wkv_hbm, wkv_ref),
                (wg_hbm, wg_ref),
                (wo_hbm, wo_ref),
            )
        )
    ]
    for load in loads:
        load.start()
    own = pltpu.make_async_copy(x_ref.at[pl.ds(col * seqs, seqs)], hx.at[col], own_sem)
    own.start()
    lax.fori_loop(1, count, greet, 0)

    key_blocks[...] = jnp.zeros_like(key_blocks)
    value_blocks[...] = jnp.zeros_like(value_blocks)
    with jax.named_scope("weights_by_owner"):
        to = lax.broadcasted_iota(jnp.int32, (both, both), 0)
        source = lax.broadcasted_iota(jnp.int32, (both, both), 1)
        wanted = (to % (2 * mine)) // mine * cz + to // (2 * mine) * mine + to % mine
        order = (source == wanted).astype(BF16)
        loads[1].wait()
        loads[2].wait()
        edge_w = [
            dot(
                order,
                jnp.concatenate(
                    [left_w_ref[:, n * cz : n * cz + cz], right_w_ref[:, n * cz : n * cz + cz]],
                    axis=1,
                ),
                ((1,), (1,)),
            ).astype(BF16)
            for n in range(2)
        ]

    pl.semaphore_wait(barrier, count - 1)
    for step in range(1, cols):
        peer = lax.rem(col + step, cols)
        pltpu.make_async_remote_copy(
            src_ref=x_ref.at[pl.ds(peer * seqs, seqs)],
            dst_ref=hx.at[col],
            send_sem=x_send_sem,
            recv_sem=x_recv_sem,
            device_id=(row, peer),
            device_id_type=MESH,
        ).start()

    with jax.named_scope("pair_bias"):
        loads[0].wait()
        pair = pair_ref[...].astype(F32).reshape(positions, cz)
        pn = normalize(pair, -1).astype(BF16)
        pn_ref[...] = pn
        bias = dot(bias_w_ref[...], pn, ((1,), (1,)))
        bias = jnp.concatenate([bias[:, :half], bias[:, half:]], axis=0).astype(BF16)
        brecv[pl.ds(col * rows + row, 1)] = bias[None]

    for step in range(1, rows):
        pltpu.make_async_remote_copy(
            src_ref=brecv.at[col * rows + row],
            dst_ref=brecv.at[col * rows + row],
            send_sem=r_send_sem,
            recv_sem=r_recv_sem,
            device_id=(lax.rem(row + step, rows), col),
            device_id_type=MESH,
        ).start()

    with jax.named_scope("pair_edges"):
        k_of = lane_blocks((1, positions), pair_cols)
        mask = jnp.zeros((1, positions), F32)
        for k in range(pair_rows):
            mask = jnp.where(k_of == k, flags_smem[row * pair_rows + k].astype(F32), mask)
        edge = (
            mask
            * jax.nn.sigmoid(dot(edge_w[0], pn, ((1,), (1,))))
            * dot(edge_w[1], pn, ((1,), (1,)))
        )
        edge = edge.reshape(count, 2 * mine, positions)
        send[...] = jnp.concatenate([edge[:, :, :half], edge[:, :, half:]], axis=1).astype(BF16)

    def push(step, carry):
        to_row, to_col = other(step)
        slot = to_row * cols + to_col
        pltpu.make_async_remote_copy(
            src_ref=send.at[slot],
            dst_ref=recv.at[me],
            send_sem=e_send_sem,
            recv_sem=e_recv_sem,
            device_id=(to_row, to_col),
            device_id_type=MESH,
        ).start()
        return carry

    lax.fori_loop(1, count, push, 0)
    recv[pl.ds(me, 1)] = send[pl.ds(me, 1)]

    def wait_for(ref, number, sem):
        part = ref.at[pl.ds(0, number)]
        pltpu.make_async_copy(part, part, sem).wait()

    wait_for(brecv, rows - 1, r_recv_sem)
    for step in range(1, cols):
        pltpu.make_async_remote_copy(
            src_ref=brecv.at[pl.ds(col * rows, rows)],
            dst_ref=brecv.at[pl.ds(col * rows, rows)],
            send_sem=c_send_sem,
            recv_sem=c_recv_sem,
            device_id=(row, lax.rem(col + step, cols)),
            device_id_type=MESH,
        ).start()

    own.wait()
    wait_for(hx, cols - 1, x_recv_sem)
    for load in loads[5:]:
        load.wait()
    with jax.named_scope("projections"):
        key_w = wkv_ref[:, :depth].astype(F32).T.astype(BF16)
        for g in range(seqs // at_once):
            x = [hx[:, g * at_once + n].reshape(total_res, depth) for n in range(at_once)]
            xn = normalize(jnp.concatenate(x, axis=0).astype(F32), -1).astype(BF16)
            q_ref[g] = (dot(xn, wq_ref[...]) * width ** (-0.5)).astype(BF16)
            k_ref[g] = dot(key_w, xn, ((1,), (1,))).astype(BF16)
            v_ref[g] = dot(xn, wkv_ref[:, depth:]).astype(BF16)
            g_ref[g] = jax.nn.sigmoid(dot(xn, wg_ref[...]))

    block = pair_cols
    lanes = total_res
    per_tile = lanes // block
    where_block = lane_blocks((16 * rows, lanes), block)

    def to_matrices(part, pieces_of):
        for tile in range(half // lanes):
            pieces = pieces_of(tile)
            for k in range(per_tile):
                merged = shift_lanes(pieces[0], (0 - k) * block)
                for c in range(1, cols):
                    merged = jnp.where(
                        where_block == c, shift_lanes(pieces[c], (c - k) * block), merged
                    )
                zed[part, pl.ds(tile * per_tile + k, 16 * rows, stride=8), :] = merged

    def edge_pieces(tile):
        taken = recv[:, :, tile * lanes : (tile + 1) * lanes]
        taken = taken.astype(F32).reshape(rows, cols, 16, lanes)
        return [taken[:, c].reshape(16 * rows, lanes) for c in range(cols)]

    def bias_pieces(tile):
        taken = brecv[:, :, tile * lanes : (tile + 1) * lanes]
        taken = taken.astype(F32).reshape(cols, 16 * rows, lanes)
        return [taken[c] for c in range(cols)]

    def matrix(part, q):
        return zed[part].reshape(2 * rows, 8, 8, lanes)[:, q].reshape(total_res, lanes)

    wait_for(recv, count - 1, e_recv_sem)
    with jax.named_scope("edge_matrices"):
        to_matrices(0, edge_pieces)
    with jax.named_scope("triangle_product"):
        for ch in range(mine):
            left = matrix(0, ch).T.astype(BF16)
            right = matrix(0, mine + ch).astype(BF16)
            product = dot(left, right).reshape(2 * rows, 8, lanes)
            zprod[:, ch] = product
        where_small = lane_blocks((2 * rows * mine, lanes), block)
        for tile in range(half // lanes):
            taken = [
                zprod.reshape(2 * rows * mine * 8, lanes)[
                    pl.ds(tile * per_tile + k, 2 * rows * mine, stride=8), :
                ]
                for k in range(per_tile)
            ]
            merged_all = []
            for c in range(cols):
                merged = shift_lanes(taken[0], (0 - c) * block)
                for k in range(1, per_tile):
                    merged = jnp.where(
                        where_small == k, shift_lanes(taken[k], (k - c) * block), merged
                    )
                merged_all.append(merged.reshape(rows, 2 * mine, lanes))
            psend[:, :, tile * lanes : (tile + 1) * lanes] = jnp.stack(
                merged_all, axis=1
            ).reshape(count, 2 * mine, lanes)

    def push_product(step, carry):
        to_row, to_col = other(step)
        slot = to_row * cols + to_col
        pltpu.make_async_remote_copy(
            src_ref=psend.at[slot],
            dst_ref=precv.at[me],
            send_sem=p_send_sem,
            recv_sem=p_recv_sem,
            device_id=(to_row, to_col),
            device_id_type=MESH,
        ).start()
        return carry

    lax.fori_loop(1, count, push_product, 0)
    precv[pl.ds(me, 1)] = psend[pl.ds(me, 1)]

    wait_for(brecv, (cols - 1) * rows, c_recv_sem)
    with jax.named_scope("attention_bias"):
        to_matrices(1, bias_pieces)
        identity = jnp.broadcast_to(identity_ref[...].astype(F32), (total_res, total_res))
        cross = (identity.T != identity).astype(F32)
        for h in range(heads):
            extra[h] = matrix(1, h) + offset_ref[h] * cross

    keep = keep_ref[...] > 0
    head_of = lane_blocks((total_res, 128), width)
    in_tile = 128 // width
    in_head = [(lane_blocks((1, 128), width) == h).astype(F32).astype(BF16) for h in range(in_tile)]

    def attend(group, n):
        here = slice(n * total_res, (n + 1) * total_res)
        for h in range(heads):
            down = slice(h * width, (h + 1) * width)
            across = slice(h * total_res, (h + 1) * total_res)
            tile = slice(h // in_tile * 128, (h // in_tile + 1) * 128)
            key_blocks[n, down, across] = k_ref[group, down, here]
            value_blocks[n, across, tile] = v_ref[group, here, tile] * in_head[h % in_tile]
        scores = dot(q_ref[group, here], key_blocks[n])
        probs = []
        totals = [jnp.ones((total_res, 128), F32)] * (depth // 128)
        for h in range(heads):
            one = scores[:, h * total_res : (h + 1) * total_res] + extra[h]
            one = jnp.where(keep, one, -1000000000.0)
            one = jnp.exp(one - jnp.max(one, axis=-1, keepdims=True))
            totals[h // in_tile] = jnp.where(
                head_of == h % in_tile, jnp.sum(one, axis=-1, keepdims=True), totals[h // in_tile]
            )
            probs.append(one.astype(BF16))
        attended = dot(jnp.concatenate(probs, axis=1), value_blocks[n])
        attended = attended / jnp.concatenate(totals, axis=1)
        gate = g_ref[group, here]
        gated = (gate * attended).astype(BF16)
        x = hx[:, group * at_once + n].reshape(total_res, depth).astype(F32)
        result = (x + dot(gated, wo_ref[...])).astype(BF16)
        return result.reshape(cols, residues, depth)

    def attend_group(group, carry):
        first = group * at_once
        results = [attend(group, n) for n in range(at_once)]
        for n in range(at_once):
            hout[:, first + n] = results[n]
        for step in range(1, cols):
            peer = lax.rem(col + step, cols)
            pltpu.make_async_remote_copy(
                src_ref=hout.at[peer, pl.ds(first, at_once)],
                dst_ref=msa_out_ref.at[pl.ds(col * seqs + first, at_once)],
                send_sem=o_send_sem,
                recv_sem=o_recv_sem,
                device_id=(row, peer),
                device_id_type=MESH,
            ).start()
        pltpu.make_async_copy(
            hout.at[col, pl.ds(first, at_once)],
            msa_out_ref.at[pl.ds(col * seqs + first, at_once)],
            keep_sem,
        ).start()
        return carry

    with jax.named_scope("row_attention"):
        lax.fori_loop(0, seqs // at_once, attend_group, 0)

    wait_for(precv, count - 1, p_recv_sem)
    loads[3].wait()
    loads[4].wait()
    with jax.named_scope("pair_update"):
        product = precv[...]
        in_half = lax.broadcasted_iota(jnp.int32, (8, half), 0) < mine

        def spread_halves(partial):
            low = jnp.sum(jnp.where(in_half, partial, 0.0), axis=0, keepdims=True)
            high = jnp.sum(jnp.where(in_half, 0.0, partial), axis=0, keepdims=True)
            return jnp.where(in_half, low, high) / channels

        center = product - spread_halves(jnp.sum(product, axis=0))[None]
        spread = spread_halves(jnp.sum(center * center, axis=0))
        norm = (center * lax.rsqrt(spread + 1e-05)[None]).reshape(count * 8, half)
        to = lax.broadcasted_iota(jnp.int32, (2 * channels, channels), 0)
        source = lax.broadcasted_iota(jnp.int32, (2 * channels, channels), 1)
        wanted = to // (2 * mine) * mine + to % mine
        final_w = dot((source == wanted).astype(BF16), tri_out_w_ref[...])
        low_rows = to % (2 * mine) < mine
        final_w = jnp.concatenate(
            [jnp.where(low_rows, final_w, 0.0), jnp.where(low_rows, 0.0, final_w)], axis=1
        ).astype(BF16)
        update = dot(norm.T.astype(BF16), final_w)
        update = jnp.concatenate([update[:, :cz], update[:, cz:]], axis=0)
        tri_gate = jax.nn.sigmoid(dot(pn_ref[...], tri_gate_w_ref[...]))
        pair = pair_ref[...].astype(F32).reshape(positions, cz)
        pair_out_ref[...] = (
            (pair + tri_gate * update).astype(BF16).reshape(pair_rows, pair_cols, cz)
        )

    wait_for(hx, cols - 1, x_send_sem)
    wait_for(send, count - 1, e_send_sem)
    wait_for(psend, count - 1, p_send_sem)
    wait_for(brecv, rows - 1, r_send_sem)
    wait_for(brecv, (cols - 1) * rows, c_send_sem)
    wait_for(hout, cols - 1, o_send_sem)
    wait_for(hout, cols - 1, o_recv_sem)
    wait_for(hout, 1, keep_sem)


def deliver(msa_ref, pair_ref, msa_out_ref, pair_out_ref, sem):
    part = msa_ref.shape[0] // 4
    copies = [
        pltpu.make_async_copy(
            msa_ref.at[pl.ds(n * part, part)], msa_out_ref.at[pl.ds(n * part, part)], sem.at[n]
        )
        for n in range(4)
    ] + [pltpu.make_async_copy(pair_ref, pair_out_ref, sem.at[4])]
    for copy in copies:
        copy.start()
    for copy in copies:
        copy.wait()


def local_fused(
    rows,
    cols,
    homolog_tensor,
    pairwise_tensor,
    genuine_amino_flags,
    polymer_identity,
    asking_weights,
    attend_sigmoid_weights,
    lookup_content_weights,
    attend_final_weights,
    pairwise_logit_weights,
    crosspolymer_offset,
    outgoing_link_weights,
    incoming_link_weights,
    trimult_sigmoid_weights,
    trimult_final_weights,
):
    count = rows * cols
    homologs, residues, depth = homolog_tensor.shape
    pair_rows, pair_cols, cz = pairwise_tensor.shape
    heads = pairwise_logit_weights.shape[1]
    total_res = cols * residues
    seqs = homologs // cols
    mine = cz // count
    half = pair_rows * pair_cols // 2
    vmem = pl.BlockSpec(memory_space=pltpu.VMEM)
    smem = pl.BlockSpec(memory_space=pltpu.SMEM)
    hbm = pl.BlockSpec(memory_space=pltpu.HBM)
    dma = pltpu.SemaphoreType.DMA
    msa_block = (cols, seqs, residues, depth)
    results = pl.pallas_call(
        functools.partial(fused, (rows, cols, heads, cz)),
        out_shape=(
            jax.ShapeDtypeStruct(homolog_tensor.shape, BF16),
            jax.ShapeDtypeStruct(pairwise_tensor.shape, BF16),
        ),
        in_specs=[hbm, hbm, smem, vmem, vmem, smem] + [hbm] * 4 + [vmem] + [hbm] * 4,
        out_specs=(hbm, vmem),
        scratch_shapes=[
            pltpu.VMEM(msa_block, BF16),
            pltpu.VMEM(msa_block, BF16),
            pltpu.VMEM((count, 16, half), BF16),
            pltpu.VMEM((count, 16, half), BF16),
            pltpu.VMEM((count, 16, half), BF16),
            pltpu.VMEM((count, 2 * mine, half), F32),
            pltpu.VMEM((count, 2 * mine, half), F32),
            pltpu.VMEM((2, 8 * total_res, total_res), F32),
            pltpu.VMEM((2 * rows, mine, 8, total_res), F32),
            pltpu.VMEM((heads, total_res, total_res), F32),
            pltpu.VMEM((pair_rows * pair_cols, cz), BF16),
            pltpu.VMEM((seqs // 2, 2 * total_res, depth), BF16),
            pltpu.VMEM((seqs // 2, depth, 2 * total_res), BF16),
            pltpu.VMEM((seqs // 2, 2 * total_res, depth), BF16),
            pltpu.VMEM((seqs // 2, 2 * total_res, depth), F32),
            pltpu.VMEM((2, depth, heads * total_res), BF16),
            pltpu.VMEM((2, heads * total_res, depth), BF16),
            pltpu.VMEM((pair_rows, pair_cols, cz), BF16),
            pltpu.VMEM(asking_weights.shape, BF16),
            pltpu.VMEM(attend_sigmoid_weights.shape, BF16),
            pltpu.VMEM(lookup_content_weights.shape, BF16),
            pltpu.VMEM(attend_final_weights.shape, BF16),
            pltpu.VMEM(outgoing_link_weights.shape, BF16),
            pltpu.VMEM(incoming_link_weights.shape, BF16),
            pltpu.VMEM(trimult_sigmoid_weights.shape, BF16),
            pltpu.VMEM(trimult_final_weights.shape, BF16),
            dma((9,)),
        ]
        + [dma] * 14,
        compiler_params=pltpu.CompilerParams(
            collective_id=0, has_side_effects=True, vmem_limit_bytes=62 * 2**20
        ),
    )(
        homolog_tensor,
        pairwise_tensor,
        genuine_amino_flags,
        genuine_amino_flags.reshape(1, -1),
        polymer_identity.reshape(1, -1),
        crosspolymer_offset,
        asking_weights,
        attend_sigmoid_weights,
        lookup_content_weights,
        attend_final_weights,
        jnp.transpose(pairwise_logit_weights),
        outgoing_link_weights,
        incoming_link_weights,
        trimult_sigmoid_weights,
        trimult_final_weights,
    )
    return pl.pallas_call(
        deliver,
        out_shape=tuple(jax.ShapeDtypeStruct(r.shape, r.dtype) for r in results),
        in_specs=[hbm, hbm],
        out_specs=(hbm, hbm),
        scratch_shapes=[dma((5,))],
        compiler_params=pltpu.CompilerParams(vmem_limit_bytes=62 * 2**20),
    )(*results)


def from_root(array, axis, root):
    mine = lax.axis_index(axis) == root
    return lax.psum(jnp.where(mine, array, jnp.zeros_like(array)), axis)


def standardize_features(tensor):
    tensor = tensor.astype(jnp.float32)
    center = tensor - jnp.mean(tensor, axis=-1, keepdims=True)
    spread = jnp.mean(center * center, axis=-1, keepdims=True)
    return center * lax.rsqrt(spread + 1e-05)


def edges(pair_norm, weight, mask_rows, width):
    projected = jnp.dot(pair_norm, weight, preferred_element_type=jnp.float32)
    edge_vals = (
        mask_rows * jax.nn.sigmoid(projected[..., :width]) * projected[..., width:]
    ).astype(jnp.bfloat16)
    return jnp.transpose(edge_vals, (2, 0, 1))


def local(
    homolog_tensor,
    pairwise_tensor,
    genuine_amino_flags,
    polymer_identity,
    asking_weights,
    attend_sigmoid_weights,
    lookup_content_weights,
    attend_final_weights,
    pairwise_logit_weights,
    crosspolymer_offset,
    outgoing_link_weights,
    incoming_link_weights,
    trimult_sigmoid_weights,
    trimult_final_weights,
):
    row_count = lax.axis_size("row")
    col_count = lax.axis_size("col")
    row_index = lax.axis_index("row")
    col_index = lax.axis_index("col")
    homolog_entries, amino_positions, feature_depth = homolog_tensor.shape
    res_rows = pairwise_tensor.shape[0]
    pair_width = pairwise_tensor.shape[2]
    row_ratio = row_count // col_count
    head_count = pairwise_logit_weights.shape[1]
    inner_width = asking_weights.shape[1]
    per_head_width = inner_width // head_count
    standardized_homologs = standardize_features(homolog_tensor).astype(jnp.bfloat16)
    pair_norm = standardize_features(pairwise_tensor).astype(jnp.bfloat16)
    local_bias = jnp.einsum(
        "ijc,ch->hij", pair_norm, pairwise_logit_weights, preferred_element_type=jnp.float32
    ).astype(jnp.bfloat16)
    row_bias = lax.all_gather(local_bias, "col", axis=2, tiled=True)
    queries = (
        jnp.dot(standardized_homologs, asking_weights, preferred_element_type=jnp.float32)
        * per_head_width ** (-0.5)
    ).astype(jnp.bfloat16)
    queries = queries.reshape(homolog_entries, amino_positions, head_count, per_head_width)
    gate_activation = jax.nn.sigmoid(
        jnp.dot(standardized_homologs, attend_sigmoid_weights, preferred_element_type=jnp.float32)
    )
    all_bias = lax.all_gather(row_bias, "row", axis=1, tiled=True)
    bias_block = lax.dynamic_slice_in_dim(all_bias, col_index * amino_positions, amino_positions, 1)
    query_chain = lax.dynamic_slice_in_dim(
        polymer_identity, col_index * amino_positions, amino_positions, 0
    )
    cross_chain = (query_chain[:, None] != polymer_identity[None, :]).astype(jnp.float32)
    extra_bias = (
        bias_block.astype(jnp.float32) + crosspolymer_offset[:, None, None] * cross_chain[None]
    )
    keep_all = genuine_amino_flags > 0
    key_value = jnp.dot(
        lax.all_gather(standardized_homologs, "col", axis=1, tiled=True),
        lookup_content_weights,
        preferred_element_type=jnp.float32,
    ).astype(jnp.bfloat16)
    piece_len = key_value.shape[1]
    key_rows = key_value[..., :inner_width].reshape(
        homolog_entries, piece_len, head_count, per_head_width
    )
    value_rows = key_value[..., inner_width:].reshape(
        homolog_entries, piece_len, head_count, per_head_width
    )
    scores = jnp.einsum("sqhd,skhd->shqk", queries, key_rows, preferred_element_type=jnp.float32)
    scores = scores + extra_bias[None]
    scores = jnp.where(keep_all, scores, -1000000000.0)
    peak_old = jnp.full((homolog_entries, head_count, amino_positions), -jnp.inf, jnp.float32)
    total_old = jnp.zeros((homolog_entries, head_count, amino_positions), jnp.float32)
    accum_old = jnp.zeros(
        (homolog_entries, head_count, amino_positions, per_head_width), jnp.float32
    )
    peak_now = jnp.max(scores, axis=-1)
    factor = jnp.exp(peak_old - peak_now)
    exp_scores = jnp.exp(scores - peak_now[..., None])
    total_now = total_old * factor + jnp.sum(exp_scores, axis=-1)
    accum_now = accum_old * factor[..., None] + jnp.einsum(
        "shqk,skhd->shqd",
        exp_scores.astype(jnp.bfloat16),
        value_rows,
        preferred_element_type=jnp.float32,
    )
    peak_now, total_now, accum_now = (peak_now, total_now, accum_now)
    attended = accum_now / total_now[..., None]
    attended = jnp.transpose(attended, (0, 2, 1, 3)).reshape(
        homolog_entries, amino_positions, inner_width
    )
    gated_output = (gate_activation * attended).astype(jnp.bfloat16)
    attended_homologs = (
        homolog_tensor.astype(jnp.float32)
        + jnp.dot(gated_output, attend_final_weights, preferred_element_type=jnp.float32)
    ).astype(jnp.bfloat16)
    mask_rows = lax.dynamic_slice_in_dim(
        genuine_amino_flags, row_index * res_rows, res_rows, 0
    ).astype(jnp.float32)[:, None, None]
    left_tri = edges(pair_norm, outgoing_link_weights, mask_rows, pair_width)
    right_tri = edges(pair_norm, incoming_link_weights, mask_rows, pair_width)
    left_cols = lax.all_gather(left_tri, "row", axis=1, tiled=True)
    left_part = lax.dynamic_slice_in_dim(left_cols, row_index % row_ratio * res_rows, res_rows, 2)
    left_mine = from_root(left_part, "col", row_index // row_ratio)
    product = jnp.einsum(
        "cki,ckj->cij",
        left_mine,
        lax.all_gather(right_tri, "row", axis=1, tiled=True),
        preferred_element_type=jnp.float32,
    )
    product_norm = standardize_features(jnp.transpose(product, (1, 2, 0))).astype(jnp.bfloat16)
    tri_gate = jax.nn.sigmoid(
        jnp.dot(pair_norm, trimult_sigmoid_weights, preferred_element_type=jnp.float32)
    )
    update = jnp.dot(product_norm, trimult_final_weights, preferred_element_type=jnp.float32)
    pair_output = (pairwise_tensor.astype(jnp.float32) + tri_gate * update).astype(jnp.bfloat16)
    return (attended_homologs, pair_output)


def solution(mesh):
    in_specs = (
        P("row", "col", None),
        P("row", "col", None),
        P(),
        P(),
        P(),
        P(),
        P(),
        P(),
        P(),
        P(),
        P(),
        P(),
        P(),
        P(),
    )
    out_specs = (P("row", "col", None), P("row", "col", None))

    def local_either(*blocks):
        rows, cols = mesh.shape["row"], mesh.shape["col"]
        homologs, residues, depth = blocks[0].shape
        pair_rows, pair_cols, cz = blocks[1].shape
        heads = blocks[8].shape[1]
        fits = (
            cz == 4 * rows * cols
            and cz == cols * residues
            and cz == rows * pair_rows
            and pair_cols == residues == 32
            and pair_rows == 16
            and heads == 8
            and homologs % (2 * cols) == 0
            and blocks[4].shape[1] == depth
            and depth % 128 == 0
        )
        if fits:
            return local_fused(rows, cols, *blocks)
        return local(*blocks)

    return jax.shard_map(local_either, mesh=mesh, in_specs=in_specs, out_specs=out_specs, check_vma=False)
```

```python
import functools

import jax
import jax.numpy as jnp
from jax import lax
from jax.experimental import pallas as pl
from jax.experimental.pallas import tpu as pltpu
from jax.sharding import PartitionSpec as P

MESH = pl.DeviceIdType.MESH
F32 = jnp.float32
BF16 = jnp.bfloat16


def dot(a, b, contract=((1,), (0,))):
    return lax.dot_general(a, b, (contract, ((), ())), preferred_element_type=F32)


def normalize(x, axis):
    center = x - jnp.mean(x, axis=axis, keepdims=True)
    spread = jnp.mean(center * center, axis=axis, keepdims=True)
    return center * lax.rsqrt(spread + 1e-05)


def lane_blocks(shape, width):
    return lax.broadcasted_iota(jnp.int32, shape, len(shape) - 1) // width


def shift_lanes(x, amount):
    amount = amount % x.shape[-1]
    return x if amount == 0 else pltpu.roll(x, amount, x.ndim - 1)


def fused(
    dims,
    x_ref,
    pair_hbm,
    flags_smem,
    keep_ref,
    identity_ref,
    offset_ref,
    wq_hbm,
    wg_hbm,
    wkv_hbm,
    wo_hbm,
    bias_w_ref,
    left_w_hbm,
    right_w_hbm,
    tri_gate_w_hbm,
    tri_out_w_hbm,
    msa_out_ref,
    pair_out_ref,
    hx,
    hout,
    send,
    landed,
    recv,
    brecv,
    psend,
    planded,
    precv,
    zed,
    zprod,
    extra,
    pn_ref,
    q_ref,
    k_ref,
    v_ref,
    g_ref,
    key_blocks,
    value_blocks,
    pair_ref,
    wq_ref,
    wg_ref,
    wkv_ref,
    wo_ref,
    left_w_ref,
    right_w_ref,
    tri_gate_w_ref,
    tri_out_w_ref,
    in_sem,
    own_sem,
    x_send_sem,
    x_recv_sem,
    e_send_sem,
    e_recv_sem,
    p_send_sem,
    p_recv_sem,
    o_send_sem,
    o_recv_sem,
    r_send_sem,
    r_recv_sem,
    c_send_sem,
    c_recv_sem,
    keep_sem,
    f_send_sem,
    f_recv_sem,
    s_send_sem,
    s_recv_sem,
):
    rows, cols, heads, channels = dims
    count = rows * cols
    mine = channels // count
    row = lax.axis_index("row")
    col = lax.axis_index("col")
    me = row * cols + col
    seqs, residues, depth = hx.shape[1:]
    total_res = cols * residues
    width = depth // heads
    pair_rows, pair_cols, cz = pair_ref.shape
    positions = pair_rows * pair_cols
    half = positions // 2
    at_once = key_blocks.shape[0]
    both = 2 * cz

    barrier = pltpu.get_barrier_semaphore()
    row_peers = [(lax.rem(row + step, rows), col) for step in range(1, rows)]
    col_peers = [(row, lax.rem(col + step, cols)) for step in range(1, cols)]

    loads = [
        pltpu.make_async_copy(source, target, in_sem.at[n])
        for n, (source, target) in enumerate(
            (
                (pair_hbm, pair_ref),
                (left_w_hbm, left_w_ref),
                (right_w_hbm, right_w_ref),
                (tri_out_w_hbm, tri_out_w_ref),
                (tri_gate_w_hbm, tri_gate_w_ref),
                (wq_hbm, wq_ref),
                (wkv_hbm, wkv_ref),
                (wg_hbm, wg_ref),
                (wo_hbm, wo_ref),
            )
        )
    ]
    for load in loads:
        load.start()
    own = pltpu.make_async_copy(x_ref.at[pl.ds(col * seqs, seqs)], hx.at[col], own_sem)
    own.start()
    for peer in row_peers + col_peers:
        pl.semaphore_signal(barrier, inc=1, device_id=peer, device_id_type=MESH)

    key_blocks[...] = jnp.zeros_like(key_blocks)
    value_blocks[...] = jnp.zeros_like(value_blocks)
    with jax.named_scope("weights_by_owner"):
        to = lax.broadcasted_iota(jnp.int32, (both, both), 0)
        source = lax.broadcasted_iota(jnp.int32, (both, both), 1)
        wanted = (to % (2 * mine)) // mine * cz + to // (2 * mine) * mine + to % mine
        order = (source == wanted).astype(BF16)
        loads[1].wait()
        loads[2].wait()
        edge_w = [
            dot(
                order,
                jnp.concatenate(
                    [left_w_ref[:, n * cz : n * cz + cz], right_w_ref[:, n * cz : n * cz + cz]],
                    axis=1,
                ),
                ((1,), (1,)),
            ).astype(BF16)
            for n in range(2)
        ]

    pl.semaphore_wait(barrier, rows + cols - 2)
    for step in range(1, cols):
        peer = lax.rem(col + step, cols)
        pltpu.make_async_remote_copy(
            src_ref=x_ref.at[pl.ds(peer * seqs, seqs)],
            dst_ref=hx.at[col],
            send_sem=x_send_sem,
            recv_sem=x_recv_sem,
            device_id=(row, peer),
            device_id_type=MESH,
        ).start()

    with jax.named_scope("pair_bias"):
        loads[0].wait()
        pair = pair_ref[...].astype(F32).reshape(positions, cz)
        pn = normalize(pair, -1).astype(BF16)
        pn_ref[...] = pn
        bias = dot(bias_w_ref[...], pn, ((1,), (1,)))
        bias = jnp.concatenate([bias[:, :half], bias[:, half:]], axis=0).astype(BF16)
        brecv[pl.ds(col * rows + row, 1)] = bias[None]

    for step in range(1, rows):
        pltpu.make_async_remote_copy(
            src_ref=brecv.at[col * rows + row],
            dst_ref=brecv.at[col * rows + row],
            send_sem=r_send_sem,
            recv_sem=r_recv_sem,
            device_id=(lax.rem(row + step, rows), col),
            device_id_type=MESH,
        ).start()

    with jax.named_scope("pair_edges"):
        k_of = lane_blocks((1, positions), pair_cols)
        mask = jnp.zeros((1, positions), F32)
        for k in range(pair_rows):
            mask = jnp.where(k_of == k, flags_smem[row * pair_rows + k].astype(F32), mask)
        edge = (
            mask
            * jax.nn.sigmoid(dot(edge_w[0], pn, ((1,), (1,))))
            * dot(edge_w[1], pn, ((1,), (1,)))
        )
        edge = edge.reshape(count, 2 * mine, positions)
        edge = jnp.concatenate([edge[:, :, :half], edge[:, :, half:]], axis=1)
        send[...] = edge.astype(BF16).reshape(send.shape)

    def along_row(source, landing, send_sem, recv_sem):
        for peer in row_peers:
            pltpu.make_async_remote_copy(
                src_ref=source.at[peer[0]],
                dst_ref=landing.at[row],
                send_sem=send_sem,
                recv_sem=recv_sem,
                device_id=peer,
                device_id_type=MESH,
            ).start()
        landing[pl.ds(row, 1)] = source[pl.ds(row, 1)]

    def along_col(landing, target, send_sem, recv_sem):
        for peer in col_peers:
            pltpu.make_async_remote_copy(
                src_ref=landing.at[:, peer[1]],
                dst_ref=target.at[col],
                send_sem=send_sem,
                recv_sem=recv_sem,
                device_id=peer,
                device_id_type=MESH,
            ).start()
        target[pl.ds(col, 1)] = landing[:, pl.ds(col, 1)].reshape((1,) + target.shape[1:])

    along_row(send, landed, e_send_sem, e_recv_sem)

    def wait_for(ref, number, sem):
        part = ref.at[pl.ds(0, number)]
        pltpu.make_async_copy(part, part, sem).wait()

    wait_for(brecv, rows - 1, r_recv_sem)
    for step in range(1, cols):
        pltpu.make_async_remote_copy(
            src_ref=brecv.at[pl.ds(col * rows, rows)],
            dst_ref=brecv.at[pl.ds(col * rows, rows)],
            send_sem=c_send_sem,
            recv_sem=c_recv_sem,
            device_id=(row, lax.rem(col + step, cols)),
            device_id_type=MESH,
        ).start()

    wait_for(landed, rows - 1, e_recv_sem)
    along_col(landed, recv, f_send_sem, f_recv_sem)
    own.wait()
    wait_for(hx, cols - 1, x_recv_sem)
    for load in loads[5:]:
        load.wait()
    with jax.named_scope("projections"):
        key_w = wkv_ref[:, :depth].astype(F32).T.astype(BF16)
        for g in range(seqs // at_once):
            x = [hx[:, g * at_once + n].reshape(total_res, depth) for n in range(at_once)]
            xn = normalize(jnp.concatenate(x, axis=0).astype(F32), -1).astype(BF16)
            q_ref[g] = (dot(xn, wq_ref[...]) * width ** (-0.5)).astype(BF16)
            k_ref[g] = dot(key_w, xn, ((1,), (1,))).astype(BF16)
            v_ref[g] = dot(xn, wkv_ref[:, depth:]).astype(BF16)
            g_ref[g] = jax.nn.sigmoid(dot(xn, wg_ref[...]))

    block = pair_cols
    lanes = total_res
    per_tile = lanes // block
    where_block = lane_blocks((16 * rows, lanes), block)

    def to_matrices(part, pieces_of):
        for tile in range(half // lanes):
            pieces = pieces_of(tile)
            for k in range(per_tile):
                merged = shift_lanes(pieces[0], (0 - k) * block)
                for c in range(1, cols):
                    merged = jnp.where(
                        where_block == c, shift_lanes(pieces[c], (c - k) * block), merged
                    )
                zed[part, pl.ds(tile * per_tile + k, 16 * rows, stride=8), :] = merged

    def edge_pieces(tile):
        taken = recv[:, :, :, tile * lanes : (tile + 1) * lanes].astype(F32)
        return [taken[c].reshape(16 * rows, lanes) for c in range(cols)]

    def bias_pieces(tile):
        taken = brecv[:, :, tile * lanes : (tile + 1) * lanes]
        taken = taken.astype(F32).reshape(cols, 16 * rows, lanes)
        return [taken[c] for c in range(cols)]

    def matrix(part, q):
        return zed[part].reshape(2 * rows, 8, 8, lanes)[:, q].reshape(total_res, lanes)

    wait_for(recv, cols - 1, f_recv_sem)
    with jax.named_scope("edge_matrices"):
        to_matrices(0, edge_pieces)
    with jax.named_scope("triangle_product"):
        for ch in range(mine):
            left = matrix(0, ch).T.astype(BF16)
            right = matrix(0, mine + ch).astype(BF16)
            product = dot(left, right).reshape(2 * rows, 8, lanes)
            zprod[:, ch] = product
        where_small = lane_blocks((2 * rows * mine, lanes), block)
        for tile in range(half // lanes):
            taken = [
                zprod.reshape(2 * rows * mine * 8, lanes)[
                    pl.ds(tile * per_tile + k, 2 * rows * mine, stride=8), :
                ]
                for k in range(per_tile)
            ]
            merged_all = []
            for c in range(cols):
                merged = shift_lanes(taken[0], (0 - c) * block)
                for k in range(1, per_tile):
                    merged = jnp.where(
                        where_small == k, shift_lanes(taken[k], (k - c) * block), merged
                    )
                merged_all.append(merged.reshape(rows, 2 * mine, lanes))
            psend[:, :, :, tile * lanes : (tile + 1) * lanes] = jnp.stack(
                merged_all, axis=1
            )

    along_row(psend, planded, p_send_sem, p_recv_sem)

    wait_for(brecv, (cols - 1) * rows, c_recv_sem)
    with jax.named_scope("attention_bias"):
        to_matrices(1, bias_pieces)
        identity = jnp.broadcast_to(identity_ref[...].astype(F32), (total_res, total_res))
        cross = (identity.T != identity).astype(F32)
        for h in range(heads):
            extra[h] = matrix(1, h) + offset_ref[h] * cross

    keep = keep_ref[...] > 0
    head_of = lane_blocks((total_res, 128), width)
    in_tile = 128 // width
    in_head = [(lane_blocks((1, 128), width) == h).astype(F32).astype(BF16) for h in range(in_tile)]

    def attend(group, n):
        here = slice(n * total_res, (n + 1) * total_res)
        for h in range(heads):
            down = slice(h * width, (h + 1) * width)
            across = slice(h * total_res, (h + 1) * total_res)
            tile = slice(h // in_tile * 128, (h // in_tile + 1) * 128)
            key_blocks[n, down, across] = k_ref[group, down, here]
            value_blocks[n, across, tile] = v_ref[group, here, tile] * in_head[h % in_tile]
        scores = dot(q_ref[group, here], key_blocks[n])
        probs = []
        totals = [jnp.ones((total_res, 128), F32)] * (depth // 128)
        for h in range(heads):
            one = scores[:, h * total_res : (h + 1) * total_res] + extra[h]
            one = jnp.where(keep, one, -1000000000.0)
            one = jnp.exp(one - jnp.max(one, axis=-1, keepdims=True))
            totals[h // in_tile] = jnp.where(
                head_of == h % in_tile, jnp.sum(one, axis=-1, keepdims=True), totals[h // in_tile]
            )
            probs.append(one.astype(BF16))
        attended = dot(jnp.concatenate(probs, axis=1), value_blocks[n])
        attended = attended / jnp.concatenate(totals, axis=1)
        gate = g_ref[group, here]
        gated = (gate * attended).astype(BF16)
        x = hx[:, group * at_once + n].reshape(total_res, depth).astype(F32)
        result = (x + dot(gated, wo_ref[...])).astype(BF16)
        return result.reshape(cols, residues, depth)

    def attend_group(group, carry):
        first = group * at_once
        results = [attend(group, n) for n in range(at_once)]
        for n in range(at_once):
            hout[:, first + n] = results[n]
        for step in range(1, cols):
            peer = lax.rem(col + step, cols)
            pltpu.make_async_remote_copy(
                src_ref=hout.at[peer, pl.ds(first, at_once)],
                dst_ref=msa_out_ref.at[pl.ds(col * seqs + first, at_once)],
                send_sem=o_send_sem,
                recv_sem=o_recv_sem,
                device_id=(row, peer),
                device_id_type=MESH,
            ).start()
        pltpu.make_async_copy(
            hout.at[col, pl.ds(first, at_once)],
            msa_out_ref.at[pl.ds(col * seqs + first, at_once)],
            keep_sem,
        ).start()
        return carry

    with jax.named_scope("row_attention"):
        lax.fori_loop(0, seqs // at_once // 2, attend_group, 0)

    wait_for(planded, rows - 1, p_recv_sem)
    along_col(planded, precv, s_send_sem, s_recv_sem)
    with jax.named_scope("row_attention"):
        lax.fori_loop(seqs // at_once // 2, seqs // at_once, attend_group, 0)

    wait_for(precv, cols - 1, s_recv_sem)
    loads[3].wait()
    loads[4].wait()
    with jax.named_scope("pair_update"):
        product = precv[...].reshape(count, 2 * mine, half)
        in_half = lax.broadcasted_iota(jnp.int32, (8, half), 0) < mine

        def spread_halves(partial):
            low = jnp.sum(jnp.where(in_half, partial, 0.0), axis=0, keepdims=True)
            high = jnp.sum(jnp.where(in_half, 0.0, partial), axis=0, keepdims=True)
            return jnp.where(in_half, low, high) / channels

        center = product - spread_halves(jnp.sum(product, axis=0))[None]
        spread = spread_halves(jnp.sum(center * center, axis=0))
        norm = (center * lax.rsqrt(spread + 1e-05)[None]).reshape(count * 8, half)
        to = lax.broadcasted_iota(jnp.int32, (2 * channels, channels), 0)
        source = lax.broadcasted_iota(jnp.int32, (2 * channels, channels), 1)
        slot = to // (2 * mine)
        wanted = (slot % rows * cols + slot // rows) * mine + to % mine
        final_w = dot((source == wanted).astype(BF16), tri_out_w_ref[...])
        low_rows = to % (2 * mine) < mine
        final_w = jnp.concatenate(
            [jnp.where(low_rows, final_w, 0.0), jnp.where(low_rows, 0.0, final_w)], axis=1
        ).astype(BF16)
        update = dot(norm.T.astype(BF16), final_w)
        update = jnp.concatenate([update[:, :cz], update[:, cz:]], axis=0)
        tri_gate = jax.nn.sigmoid(dot(pn_ref[...], tri_gate_w_ref[...]))
        pair = pair_ref[...].astype(F32).reshape(positions, cz)
        pair_out_ref[...] = (
            (pair + tri_gate * update).astype(BF16).reshape(pair_rows, pair_cols, cz)
        )

    wait_for(hx, cols - 1, x_send_sem)
    wait_for(send, rows - 1, e_send_sem)
    wait_for(psend, rows - 1, p_send_sem)
    wait_for(recv, cols - 1, f_send_sem)
    wait_for(precv, cols - 1, s_send_sem)
    wait_for(brecv, rows - 1, r_send_sem)
    wait_for(brecv, (cols - 1) * rows, c_send_sem)
    wait_for(hout, cols - 1, o_send_sem)
    wait_for(hout, cols - 1, o_recv_sem)
    wait_for(hout, 1, keep_sem)


def deliver(msa_ref, pair_ref, msa_out_ref, pair_out_ref, msa_vmem, pair_vmem, in_sem, out_sem):
    part = msa_ref.shape[0] // 4
    moves = [
        (
            msa_ref.at[pl.ds(n * part, part)],
            msa_vmem.at[pl.ds(n * part, part)],
            msa_out_ref.at[pl.ds(n * part, part)],
        )
        for n in range(4)
    ] + [(pair_ref, pair_vmem, pair_out_ref)]
    loads = [pltpu.make_async_copy(a, b, in_sem.at[n]) for n, (a, b, _) in enumerate(moves)]
    stores = [pltpu.make_async_copy(b, c, out_sem.at[n]) for n, (_, b, c) in enumerate(moves)]
    for load in loads:
        load.start()
    for load, store in zip(loads, stores):
        load.wait()
        store.start()
    for store in stores:
        store.wait()


def local_fused(
    rows,
    cols,
    homolog_tensor,
    pairwise_tensor,
    genuine_amino_flags,
    polymer_identity,
    asking_weights,
    attend_sigmoid_weights,
    lookup_content_weights,
    attend_final_weights,
    pairwise_logit_weights,
    crosspolymer_offset,
    outgoing_link_weights,
    incoming_link_weights,
    trimult_sigmoid_weights,
    trimult_final_weights,
):
    count = rows * cols
    homologs, residues, depth = homolog_tensor.shape
    pair_rows, pair_cols, cz = pairwise_tensor.shape
    heads = pairwise_logit_weights.shape[1]
    total_res = cols * residues
    seqs = homologs // cols
    mine = cz // count
    half = pair_rows * pair_cols // 2
    vmem = pl.BlockSpec(memory_space=pltpu.VMEM)
    smem = pl.BlockSpec(memory_space=pltpu.SMEM)
    hbm = pl.BlockSpec(memory_space=pltpu.HBM)
    dma = pltpu.SemaphoreType.DMA
    msa_block = (cols, seqs, residues, depth)
    results = pl.pallas_call(
        functools.partial(fused, (rows, cols, heads, cz)),
        out_shape=(
            jax.ShapeDtypeStruct(homolog_tensor.shape, BF16),
            jax.ShapeDtypeStruct(pairwise_tensor.shape, BF16),
        ),
        in_specs=[hbm, hbm, smem, vmem, vmem, smem] + [hbm] * 4 + [vmem] + [hbm] * 4,
        out_specs=(hbm, vmem),
        scratch_shapes=[
            pltpu.VMEM(msa_block, BF16),
            pltpu.VMEM(msa_block, BF16),
            pltpu.VMEM((rows, cols, 16, half), BF16),
            pltpu.VMEM((rows, cols, 16, half), BF16),
            pltpu.VMEM((cols, rows, 16, half), BF16),
            pltpu.VMEM((count, 16, half), BF16),
            pltpu.VMEM((rows, cols, 2 * mine, half), F32),
            pltpu.VMEM((rows, cols, 2 * mine, half), F32),
            pltpu.VMEM((cols, rows, 2 * mine, half), F32),
            pltpu.VMEM((2, 8 * total_res, total_res), F32),
            pltpu.VMEM((2 * rows, mine, 8, total_res), F32),
            pltpu.VMEM((heads, total_res, total_res), F32),
            pltpu.VMEM((pair_rows * pair_cols, cz), BF16),
            pltpu.VMEM((seqs // 2, 2 * total_res, depth), BF16),
            pltpu.VMEM((seqs // 2, depth, 2 * total_res), BF16),
            pltpu.VMEM((seqs // 2, 2 * total_res, depth), BF16),
            pltpu.VMEM((seqs // 2, 2 * total_res, depth), F32),
            pltpu.VMEM((2, depth, heads * total_res), BF16),
            pltpu.VMEM((2, heads * total_res, depth), BF16),
            pltpu.VMEM((pair_rows, pair_cols, cz), BF16),
            pltpu.VMEM(asking_weights.shape, BF16),
            pltpu.VMEM(attend_sigmoid_weights.shape, BF16),
            pltpu.VMEM(lookup_content_weights.shape, BF16),
            pltpu.VMEM(attend_final_weights.shape, BF16),
            pltpu.VMEM(outgoing_link_weights.shape, BF16),
            pltpu.VMEM(incoming_link_weights.shape, BF16),
            pltpu.VMEM(trimult_sigmoid_weights.shape, BF16),
            pltpu.VMEM(trimult_final_weights.shape, BF16),
            dma((9,)),
        ]
        + [dma] * 18,
        compiler_params=pltpu.CompilerParams(
            collective_id=0, has_side_effects=True, vmem_limit_bytes=62 * 2**20
        ),
    )(
        homolog_tensor,
        pairwise_tensor,
        genuine_amino_flags,
        genuine_amino_flags.reshape(1, -1),
        polymer_identity.reshape(1, -1),
        crosspolymer_offset,
        asking_weights,
        attend_sigmoid_weights,
        lookup_content_weights,
        attend_final_weights,
        jnp.transpose(pairwise_logit_weights),
        outgoing_link_weights,
        incoming_link_weights,
        trimult_sigmoid_weights,
        trimult_final_weights,
    )
    return pl.pallas_call(
        deliver,
        out_shape=tuple(jax.ShapeDtypeStruct(r.shape, r.dtype) for r in results),
        in_specs=[hbm, hbm],
        out_specs=(hbm, hbm),
        scratch_shapes=[pltpu.VMEM(r.shape, r.dtype) for r in results] + [dma((5,)), dma((5,))],
        compiler_params=pltpu.CompilerParams(vmem_limit_bytes=62 * 2**20),
    )(*results)


def from_root(array, axis, root):
    mine = lax.axis_index(axis) == root
    return lax.psum(jnp.where(mine, array, jnp.zeros_like(array)), axis)


def standardize_features(tensor):
    tensor = tensor.astype(jnp.float32)
    center = tensor - jnp.mean(tensor, axis=-1, keepdims=True)
    spread = jnp.mean(center * center, axis=-1, keepdims=True)
    return center * lax.rsqrt(spread + 1e-05)


def edges(pair_norm, weight, mask_rows, width):
    projected = jnp.dot(pair_norm, weight, preferred_element_type=jnp.float32)
    edge_vals = (
        mask_rows * jax.nn.sigmoid(projected[..., :width]) * projected[..., width:]
    ).astype(jnp.bfloat16)
    return jnp.transpose(edge_vals, (2, 0, 1))


def local(
    homolog_tensor,
    pairwise_tensor,
    genuine_amino_flags,
    polymer_identity,
    asking_weights,
    attend_sigmoid_weights,
    lookup_content_weights,
    attend_final_weights,
    pairwise_logit_weights,
    crosspolymer_offset,
    outgoing_link_weights,
    incoming_link_weights,
    trimult_sigmoid_weights,
    trimult_final_weights,
):
    row_count = lax.axis_size("row")
    col_count = lax.axis_size("col")
    row_index = lax.axis_index("row")
    col_index = lax.axis_index("col")
    homolog_entries, amino_positions, feature_depth = homolog_tensor.shape
    res_rows = pairwise_tensor.shape[0]
    pair_width = pairwise_tensor.shape[2]
    row_ratio = row_count // col_count
    head_count = pairwise_logit_weights.shape[1]
    inner_width = asking_weights.shape[1]
    per_head_width = inner_width // head_count
    standardized_homologs = standardize_features(homolog_tensor).astype(jnp.bfloat16)
    pair_norm = standardize_features(pairwise_tensor).astype(jnp.bfloat16)
    local_bias = jnp.einsum(
        "ijc,ch->hij", pair_norm, pairwise_logit_weights, preferred_element_type=jnp.float32
    ).astype(jnp.bfloat16)
    row_bias = lax.all_gather(local_bias, "col", axis=2, tiled=True)
    queries = (
        jnp.dot(standardized_homologs, asking_weights, preferred_element_type=jnp.float32)
        * per_head_width ** (-0.5)
    ).astype(jnp.bfloat16)
    queries = queries.reshape(homolog_entries, amino_positions, head_count, per_head_width)
    gate_activation = jax.nn.sigmoid(
        jnp.dot(standardized_homologs, attend_sigmoid_weights, preferred_element_type=jnp.float32)
    )
    all_bias = lax.all_gather(row_bias, "row", axis=1, tiled=True)
    bias_block = lax.dynamic_slice_in_dim(all_bias, col_index * amino_positions, amino_positions, 1)
    query_chain = lax.dynamic_slice_in_dim(
        polymer_identity, col_index * amino_positions, amino_positions, 0
    )
    cross_chain = (query_chain[:, None] != polymer_identity[None, :]).astype(jnp.float32)
    extra_bias = (
        bias_block.astype(jnp.float32) + crosspolymer_offset[:, None, None] * cross_chain[None]
    )
    keep_all = genuine_amino_flags > 0
    key_value = jnp.dot(
        lax.all_gather(standardized_homologs, "col", axis=1, tiled=True),
        lookup_content_weights,
        preferred_element_type=jnp.float32,
    ).astype(jnp.bfloat16)
    piece_len = key_value.shape[1]
    key_rows = key_value[..., :inner_width].reshape(
        homolog_entries, piece_len, head_count, per_head_width
    )
    value_rows = key_value[..., inner_width:].reshape(
        homolog_entries, piece_len, head_count, per_head_width
    )
    scores = jnp.einsum("sqhd,skhd->shqk", queries, key_rows, preferred_element_type=jnp.float32)
    scores = scores + extra_bias[None]
    scores = jnp.where(keep_all, scores, -1000000000.0)
    peak_old = jnp.full((homolog_entries, head_count, amino_positions), -jnp.inf, jnp.float32)
    total_old = jnp.zeros((homolog_entries, head_count, amino_positions), jnp.float32)
    accum_old = jnp.zeros(
        (homolog_entries, head_count, amino_positions, per_head_width), jnp.float32
    )
    peak_now = jnp.max(scores, axis=-1)
    factor = jnp.exp(peak_old - peak_now)
    exp_scores = jnp.exp(scores - peak_now[..., None])
    total_now = total_old * factor + jnp.sum(exp_scores, axis=-1)
    accum_now = accum_old * factor[..., None] + jnp.einsum(
        "shqk,skhd->shqd",
        exp_scores.astype(jnp.bfloat16),
        value_rows,
        preferred_element_type=jnp.float32,
    )
    peak_now, total_now, accum_now = (peak_now, total_now, accum_now)
    attended = accum_now / total_now[..., None]
    attended = jnp.transpose(attended, (0, 2, 1, 3)).reshape(
        homolog_entries, amino_positions, inner_width
    )
    gated_output = (gate_activation * attended).astype(jnp.bfloat16)
    attended_homologs = (
        homolog_tensor.astype(jnp.float32)
        + jnp.dot(gated_output, attend_final_weights, preferred_element_type=jnp.float32)
    ).astype(jnp.bfloat16)
    mask_rows = lax.dynamic_slice_in_dim(
        genuine_amino_flags, row_index * res_rows, res_rows, 0
    ).astype(jnp.float32)[:, None, None]
    left_tri = edges(pair_norm, outgoing_link_weights, mask_rows, pair_width)
    right_tri = edges(pair_norm, incoming_link_weights, mask_rows, pair_width)
    left_cols = lax.all_gather(left_tri, "row", axis=1, tiled=True)
    left_part = lax.dynamic_slice_in_dim(left_cols, row_index % row_ratio * res_rows, res_rows, 2)
    left_mine = from_root(left_part, "col", row_index // row_ratio)
    product = jnp.einsum(
        "cki,ckj->cij",
        left_mine,
        lax.all_gather(right_tri, "row", axis=1, tiled=True),
        preferred_element_type=jnp.float32,
    )
    product_norm = standardize_features(jnp.transpose(product, (1, 2, 0))).astype(jnp.bfloat16)
    tri_gate = jax.nn.sigmoid(
        jnp.dot(pair_norm, trimult_sigmoid_weights, preferred_element_type=jnp.float32)
    )
    update = jnp.dot(product_norm, trimult_final_weights, preferred_element_type=jnp.float32)
    pair_output = (pairwise_tensor.astype(jnp.float32) + tri_gate * update).astype(jnp.bfloat16)
    return (attended_homologs, pair_output)


def solution(mesh):
    in_specs = (
        P("row", "col", None),
        P("row", "col", None),
        P(),
        P(),
        P(),
        P(),
        P(),
        P(),
        P(),
        P(),
        P(),
        P(),
        P(),
        P(),
    )
    out_specs = (P("row", "col", None), P("row", "col", None))

    def local_either(*blocks):
        rows, cols = mesh.shape["row"], mesh.shape["col"]
        homologs, residues, depth = blocks[0].shape
        pair_rows, pair_cols, cz = blocks[1].shape
        heads = blocks[8].shape[1]
        fits = (
            cz == 4 * rows * cols
            and cz == cols * residues
            and cz == rows * pair_rows
            and pair_cols == residues == 32
            and pair_rows == 16
            and heads == 8
            and homologs % (2 * cols) == 0
            and blocks[4].shape[1] == depth
            and depth % 128 == 0
        )
        if fits:
            return local_fused(rows, cols, *blocks)
        return local(*blocks)

    return jax.shard_map(local_either, mesh=mesh, in_specs=in_specs, out_specs=out_specs, check_vma=False)
```

```python
import functools

import jax
import jax.numpy as jnp
from jax import lax
from jax.experimental import pallas as pl
from jax.experimental.pallas import tpu as pltpu
from jax.sharding import PartitionSpec as P

MESH = pl.DeviceIdType.MESH
F32 = jnp.float32
BF16 = jnp.bfloat16


def dot(a, b, contract=((1,), (0,))):
    return lax.dot_general(a, b, (contract, ((), ())), preferred_element_type=F32)


def normalize(x, axis):
    center = x - jnp.mean(x, axis=axis, keepdims=True)
    spread = jnp.mean(center * center, axis=axis, keepdims=True)
    return center * lax.rsqrt(spread + 1e-05)


def lane_blocks(shape, width):
    return lax.broadcasted_iota(jnp.int32, shape, len(shape) - 1) // width


def shift_lanes(x, amount):
    amount = amount % x.shape[-1]
    return x if amount == 0 else pltpu.roll(x, amount, x.ndim - 1)


def fused(
    dims,
    x_ref,
    pair_hbm,
    flags_smem,
    keep_ref,
    identity_ref,
    offset_ref,
    wq_hbm,
    wg_hbm,
    wkv_hbm,
    wo_hbm,
    bias_w_ref,
    left_w_hbm,
    right_w_hbm,
    tri_gate_w_hbm,
    tri_out_w_hbm,
    msa_out_ref,
    pair_out_ref,
    hx,
    hout,
    send,
    recv,
    brecv,
    psend,
    precv,
    zed,
    zprod,
    extra,
    pn_ref,
    q_ref,
    k_ref,
    v_ref,
    g_ref,
    key_blocks,
    value_blocks,
    pair_ref,
    wq_ref,
    wg_ref,
    wkv_ref,
    wo_ref,
    left_w_ref,
    right_w_ref,
    tri_gate_w_ref,
    tri_out_w_ref,
    in_sem,
    own_sem,
    x_send_sem,
    x_recv_sem,
    e_send_sem,
    e_recv_sem,
    p_send_sem,
    p_recv_sem,
    o_send_sem,
    o_recv_sem,
    r_send_sem,
    r_recv_sem,
    c_send_sem,
    c_recv_sem,
    keep_sem,
):
    rows, cols, heads, channels = dims
    count = rows * cols
    mine = channels // count
    row = lax.axis_index("row")
    col = lax.axis_index("col")
    me = row * cols + col
    seqs, residues, depth = hx.shape[1:]
    total_res = cols * residues
    width = depth // heads
    pair_rows, pair_cols, cz = pair_ref.shape
    positions = pair_rows * pair_cols
    half = positions // 2
    at_once = key_blocks.shape[0]
    both = 2 * cz

    def other(step):
        peer = lax.rem(me + step, count)
        return peer // cols, lax.rem(peer, cols)

    barrier = pltpu.get_barrier_semaphore()

    def greet(step, carry):
        pl.semaphore_signal(barrier, inc=1, device_id=other(step), device_id_type=MESH)
        return carry

    loads = [
        pltpu.make_async_copy(source, target, in_sem.at[n])
        for n, (source, target) in enumerate(
            (
                (pair_hbm, pair_ref),
                (left_w_hbm, left_w_ref),
                (right_w_hbm, right_w_ref),
                (tri_out_w_hbm, tri_out_w_ref),
                (tri_gate_w_hbm, tri_gate_w_ref),
                (wq_hbm, wq_ref),
                (wkv_hbm, wkv_ref),
                (wg_hbm, wg_ref),
                (wo_hbm, wo_ref),
            )
        )
    ]
    for load in loads:
        load.start()
    own = pltpu.make_async_copy(x_ref.at[pl.ds(col * seqs, seqs)], hx.at[col], own_sem)
    own.start()
    lax.fori_loop(1, count, greet, 0)

    key_blocks[...] = jnp.zeros_like(key_blocks)
    value_blocks[...] = jnp.zeros_like(value_blocks)
    with jax.named_scope("weights_by_owner"):
        to = lax.broadcasted_iota(jnp.int32, (both, both), 0)
        source = lax.broadcasted_iota(jnp.int32, (both, both), 1)
        wanted = (to % (2 * mine)) // mine * cz + to // (2 * mine) * mine + to % mine
        order = (source == wanted).astype(BF16)
        loads[1].wait()
        loads[2].wait()
        edge_w = [
            dot(
                order,
                jnp.concatenate(
                    [left_w_ref[:, n * cz : n * cz + cz], right_w_ref[:, n * cz : n * cz + cz]],
                    axis=1,
                ),
                ((1,), (1,)),
            ).astype(BF16)
            for n in range(2)
        ]

    pl.semaphore_wait(barrier, count - 1)
    for step in range(1, cols):
        peer = lax.rem(col + step, cols)
        pltpu.make_async_remote_copy(
            src_ref=x_ref.at[pl.ds(peer * seqs, seqs)],
            dst_ref=hx.at[col],
            send_sem=x_send_sem,
            recv_sem=x_recv_sem.at[step],
            device_id=(row, peer),
            device_id_type=MESH,
        ).start()

    with jax.named_scope("pair_bias"):
        loads[0].wait()
        pair = pair_ref[...].astype(F32).reshape(positions, cz)
        pn = normalize(pair, -1).astype(BF16)
        pn_ref[...] = pn
        bias = dot(bias_w_ref[...], pn, ((1,), (1,)))
        bias = jnp.concatenate([bias[:, :half], bias[:, half:]], axis=0).astype(BF16)
        brecv[pl.ds(col * rows + row, 1)] = bias[None]

    for step in range(1, rows):
        pltpu.make_async_remote_copy(
            src_ref=brecv.at[col * rows + row],
            dst_ref=brecv.at[col * rows + row],
            send_sem=r_send_sem,
            recv_sem=r_recv_sem,
            device_id=(lax.rem(row + step, rows), col),
            device_id_type=MESH,
        ).start()

    with jax.named_scope("pair_edges"):
        k_of = lane_blocks((1, positions), pair_cols)
        mask = jnp.zeros((1, positions), F32)
        for k in range(pair_rows):
            mask = jnp.where(k_of == k, flags_smem[row * pair_rows + k].astype(F32), mask)
        edge = (
            mask
            * jax.nn.sigmoid(dot(edge_w[0], pn, ((1,), (1,))))
            * dot(edge_w[1], pn, ((1,), (1,)))
        )
        edge = edge.reshape(count, 2 * mine, positions)
        send[...] = jnp.concatenate([edge[:, :, :half], edge[:, :, half:]], axis=1).astype(BF16)

    def push(step, carry):
        to_row, to_col = other(step)
        slot = to_row * cols + to_col
        pltpu.make_async_remote_copy(
            src_ref=send.at[slot],
            dst_ref=recv.at[me],
            send_sem=e_send_sem,
            recv_sem=e_recv_sem,
            device_id=(to_row, to_col),
            device_id_type=MESH,
        ).start()
        return carry

    lax.fori_loop(1, count, push, 0)
    recv[pl.ds(me, 1)] = send[pl.ds(me, 1)]

    def wait_for(ref, number, sem):
        part = ref.at[pl.ds(0, number)]
        pltpu.make_async_copy(part, part, sem).wait()

    wait_for(brecv, rows - 1, r_recv_sem)
    for step in range(1, cols):
        pltpu.make_async_remote_copy(
            src_ref=brecv.at[pl.ds(col * rows, rows)],
            dst_ref=brecv.at[pl.ds(col * rows, rows)],
            send_sem=c_send_sem,
            recv_sem=c_recv_sem,
            device_id=(row, lax.rem(col + step, cols)),
            device_id_type=MESH,
        ).start()

    for load in loads[5:]:
        load.wait()
    with jax.named_scope("projections"):
        for step in range(cols):
            if step == 0:
                own.wait()
            else:
                pltpu.make_async_copy(hx.at[0], hx.at[0], x_recv_sem.at[step]).wait()
            c = lax.rem(col + cols - step, cols)
            shape = (1, seqs, residues, depth)
            x = hx[pl.ds(c, 1)].reshape(seqs * residues, depth).astype(F32)
            xn = normalize(x, -1).astype(BF16)
            queries = dot(xn, wq_ref[...]) * width ** (-0.5)
            q_ref[pl.ds(c, 1)] = queries.astype(BF16).reshape(shape)
            kv = dot(xn, wkv_ref[...]).astype(BF16)
            k_ref[pl.ds(c, 1)] = kv[:, :depth].reshape(shape)
            v_ref[pl.ds(c, 1)] = kv[:, depth:].reshape(shape)
            g_ref[pl.ds(c, 1)] = jax.nn.sigmoid(dot(xn, wg_ref[...])).reshape(shape)

    block = pair_cols
    lanes = total_res
    per_tile = lanes // block
    where_block = lane_blocks((16 * rows, lanes), block)

    def to_matrices(part, pieces_of):
        for tile in range(half // lanes):
            pieces = pieces_of(tile)
            for k in range(per_tile):
                merged = shift_lanes(pieces[0], (0 - k) * block)
                for c in range(1, cols):
                    merged = jnp.where(
                        where_block == c, shift_lanes(pieces[c], (c - k) * block), merged
                    )
                zed[part, pl.ds(tile * per_tile + k, 16 * rows, stride=8), :] = merged

    def edge_pieces(tile):
        taken = recv[:, :, tile * lanes : (tile + 1) * lanes]
        taken = taken.astype(F32).reshape(rows, cols, 16, lanes)
        return [taken[:, c].reshape(16 * rows, lanes) for c in range(cols)]

    def bias_pieces(tile):
        taken = brecv[:, :, tile * lanes : (tile + 1) * lanes]
        taken = taken.astype(F32).reshape(cols, 16 * rows, lanes)
        return [taken[c] for c in range(cols)]

    def matrix(part, q):
        return zed[part].reshape(2 * rows, 8, 8, lanes)[:, q].reshape(total_res, lanes)

    wait_for(recv, count - 1, e_recv_sem)
    with jax.named_scope("edge_matrices"):
        to_matrices(0, edge_pieces)
    with jax.named_scope("triangle_product"):
        for ch in range(mine):
            left = matrix(0, ch).T.astype(BF16)
            right = matrix(0, mine + ch).astype(BF16)
            product = dot(left, right).reshape(2 * rows, 8, lanes)
            zprod[:, ch] = product
        where_small = lane_blocks((2 * rows * mine, lanes), block)
        for tile in range(half // lanes):
            taken = [
                zprod.reshape(2 * rows * mine * 8, lanes)[
                    pl.ds(tile * per_tile + k, 2 * rows * mine, stride=8), :
                ]
                for k in range(per_tile)
            ]
            merged_all = []
            for c in range(cols):
                merged = shift_lanes(taken[0], (0 - c) * block)
                for k in range(1, per_tile):
                    merged = jnp.where(
                        where_small == k, shift_lanes(taken[k], (k - c) * block), merged
                    )
                merged_all.append(merged.reshape(rows, 2 * mine, lanes))
            psend[:, :, tile * lanes : (tile + 1) * lanes] = jnp.stack(
                merged_all, axis=1
            ).reshape(count, 2 * mine, lanes)

    def push_product(step, carry):
        to_row, to_col = other(step)
        slot = to_row * cols + to_col
        pltpu.make_async_remote_copy(
            src_ref=psend.at[slot],
            dst_ref=precv.at[me],
            send_sem=p_send_sem,
            recv_sem=p_recv_sem,
            device_id=(to_row, to_col),
            device_id_type=MESH,
        ).start()
        return carry

    lax.fori_loop(1, count, push_product, 0)
    precv[pl.ds(me, 1)] = psend[pl.ds(me, 1)]

    wait_for(brecv, (cols - 1) * rows, c_recv_sem)
    with jax.named_scope("attention_bias"):
        to_matrices(1, bias_pieces)
        identity = jnp.broadcast_to(identity_ref[...].astype(F32), (total_res, total_res))
        cross = (identity.T != identity).astype(F32)
        for h in range(heads):
            extra[h] = matrix(1, h) + offset_ref[h] * cross

    keep = keep_ref[...] > 0
    head_of = lane_blocks((total_res, 128), width)
    in_tile = 128 // width
    in_head = [(lane_blocks((1, 128), width) == h).astype(F32).astype(BF16) for h in range(in_tile)]

    def attend(group, n):
        s = group * at_once + n
        keys = k_ref[:, s].reshape(total_res, depth)
        values = v_ref[:, s].reshape(total_res, depth)
        for h in range(heads):
            down = slice(h * total_res, (h + 1) * total_res)
            tile = slice(h // in_tile * 128, (h // in_tile + 1) * 128)
            key_blocks[n, down, tile] = keys[:, tile] * in_head[h % in_tile]
            value_blocks[n, down, tile] = values[:, tile] * in_head[h % in_tile]
        queries = q_ref[:, s].reshape(total_res, depth)
        scores = dot(queries, key_blocks[n], ((1,), (1,)))
        probs = []
        totals = [jnp.ones((total_res, 128), F32)] * (depth // 128)
        for h in range(heads):
            one = scores[:, h * total_res : (h + 1) * total_res] + extra[h]
            one = jnp.where(keep, one, -1000000000.0)
            one = jnp.exp(one - jnp.max(one, axis=-1, keepdims=True))
            totals[h // in_tile] = jnp.where(
                head_of == h % in_tile, jnp.sum(one, axis=-1, keepdims=True), totals[h // in_tile]
            )
            probs.append(one.astype(BF16))
        attended = dot(jnp.concatenate(probs, axis=1), value_blocks[n])
        attended = attended / jnp.concatenate(totals, axis=1)
        gate = g_ref[:, s].reshape(total_res, depth)
        gated = (gate * attended).astype(BF16)
        x = hx[:, s].reshape(total_res, depth).astype(F32)
        result = (x + dot(gated, wo_ref[...])).astype(BF16)
        return result.reshape(cols, residues, depth)

    def attend_group(group, carry):
        first = group * at_once
        results = [attend(group, n) for n in range(at_once)]
        for n in range(at_once):
            hout[:, first + n] = results[n]
        for step in range(1, cols):
            peer = lax.rem(col + step, cols)
            pltpu.make_async_remote_copy(
                src_ref=hout.at[peer, pl.ds(first, at_once)],
                dst_ref=msa_out_ref.at[pl.ds(col * seqs + first, at_once)],
                send_sem=o_send_sem,
                recv_sem=o_recv_sem,
                device_id=(row, peer),
                device_id_type=MESH,
            ).start()
        pltpu.make_async_copy(
            hout.at[col, pl.ds(first, at_once)],
            msa_out_ref.at[pl.ds(col * seqs + first, at_once)],
            keep_sem,
        ).start()
        return carry

    with jax.named_scope("row_attention"):
        lax.fori_loop(0, seqs // at_once, attend_group, 0)

    wait_for(precv, count - 1, p_recv_sem)
    loads[3].wait()
    loads[4].wait()
    with jax.named_scope("pair_update"):
        product = precv[...]
        in_half = lax.broadcasted_iota(jnp.int32, (8, half), 0) < mine

        def spread_halves(partial):
            low = jnp.sum(jnp.where(in_half, partial, 0.0), axis=0, keepdims=True)
            high = jnp.sum(jnp.where(in_half, 0.0, partial), axis=0, keepdims=True)
            return jnp.where(in_half, low, high) / channels

        center = product - spread_halves(jnp.sum(product, axis=0))[None]
        spread = spread_halves(jnp.sum(center * center, axis=0))
        norm = (center * lax.rsqrt(spread + 1e-05)[None]).reshape(count * 8, half)
        to = lax.broadcasted_iota(jnp.int32, (2 * channels, channels), 0)
        source = lax.broadcasted_iota(jnp.int32, (2 * channels, channels), 1)
        wanted = to // (2 * mine) * mine + to % mine
        final_w = dot((source == wanted).astype(BF16), tri_out_w_ref[...])
        low_rows = to % (2 * mine) < mine
        final_w = jnp.concatenate(
            [jnp.where(low_rows, final_w, 0.0), jnp.where(low_rows, 0.0, final_w)], axis=1
        ).astype(BF16)
        update = dot(norm.T.astype(BF16), final_w)
        update = jnp.concatenate([update[:, :cz], update[:, cz:]], axis=0)
        tri_gate = jax.nn.sigmoid(dot(pn_ref[...], tri_gate_w_ref[...]))
        pair = pair_ref[...].astype(F32).reshape(positions, cz)
        pair_out_ref[...] = (
            (pair + tri_gate * update).astype(BF16).reshape(pair_rows, pair_cols, cz)
        )

    wait_for(hx, cols - 1, x_send_sem)
    wait_for(send, count - 1, e_send_sem)
    wait_for(psend, count - 1, p_send_sem)
    wait_for(brecv, rows - 1, r_send_sem)
    wait_for(brecv, (cols - 1) * rows, c_send_sem)
    wait_for(hout, cols - 1, o_send_sem)
    wait_for(hout, cols - 1, o_recv_sem)
    wait_for(hout, 1, keep_sem)


def deliver(msa_ref, pair_ref, msa_out_ref, pair_out_ref, msa_vmem, pair_vmem, in_sem, out_sem):
    part = msa_ref.shape[0] // 4
    moves = [
        (
            msa_ref.at[pl.ds(n * part, part)],
            msa_vmem.at[pl.ds(n * part, part)],
            msa_out_ref.at[pl.ds(n * part, part)],
        )
        for n in range(4)
    ] + [(pair_ref, pair_vmem, pair_out_ref)]
    loads = [pltpu.make_async_copy(a, b, in_sem.at[n]) for n, (a, b, _) in enumerate(moves)]
    stores = [pltpu.make_async_copy(b, c, out_sem.at[n]) for n, (_, b, c) in enumerate(moves)]
    for load in loads:
        load.start()
    for load, store in zip(loads, stores):
        load.wait()
        store.start()
    for store in stores:
        store.wait()


def local_fused(
    rows,
    cols,
    homolog_tensor,
    pairwise_tensor,
    genuine_amino_flags,
    polymer_identity,
    asking_weights,
    attend_sigmoid_weights,
    lookup_content_weights,
    attend_final_weights,
    pairwise_logit_weights,
    crosspolymer_offset,
    outgoing_link_weights,
    incoming_link_weights,
    trimult_sigmoid_weights,
    trimult_final_weights,
):
    count = rows * cols
    homologs, residues, depth = homolog_tensor.shape
    pair_rows, pair_cols, cz = pairwise_tensor.shape
    heads = pairwise_logit_weights.shape[1]
    total_res = cols * residues
    seqs = homologs // cols
    mine = cz // count
    half = pair_rows * pair_cols // 2
    vmem = pl.BlockSpec(memory_space=pltpu.VMEM)
    smem = pl.BlockSpec(memory_space=pltpu.SMEM)
    hbm = pl.BlockSpec(memory_space=pltpu.HBM)
    dma = pltpu.SemaphoreType.DMA
    msa_block = (cols, seqs, residues, depth)
    results = pl.pallas_call(
        functools.partial(fused, (rows, cols, heads, cz)),
        out_shape=(
            jax.ShapeDtypeStruct(homolog_tensor.shape, BF16),
            jax.ShapeDtypeStruct(pairwise_tensor.shape, BF16),
        ),
        in_specs=[hbm, hbm, smem, vmem, vmem, smem] + [hbm] * 4 + [vmem] + [hbm] * 4,
        out_specs=(hbm, vmem),
        scratch_shapes=[
            pltpu.VMEM(msa_block, BF16),
            pltpu.VMEM(msa_block, BF16),
            pltpu.VMEM((count, 16, half), BF16),
            pltpu.VMEM((count, 16, half), BF16),
            pltpu.VMEM((count, 16, half), BF16),
            pltpu.VMEM((count, 2 * mine, half), F32),
            pltpu.VMEM((count, 2 * mine, half), F32),
            pltpu.VMEM((2, 8 * total_res, total_res), F32),
            pltpu.VMEM((2 * rows, mine, 8, total_res), F32),
            pltpu.VMEM((heads, total_res, total_res), F32),
            pltpu.VMEM((pair_rows * pair_cols, cz), BF16),
            pltpu.VMEM(msa_block, BF16),
            pltpu.VMEM(msa_block, BF16),
            pltpu.VMEM(msa_block, BF16),
            pltpu.VMEM(msa_block, F32),
            pltpu.VMEM((2, heads * total_res, depth), BF16),
            pltpu.VMEM((2, heads * total_res, depth), BF16),
            pltpu.VMEM((pair_rows, pair_cols, cz), BF16),
            pltpu.VMEM(asking_weights.shape, BF16),
            pltpu.VMEM(attend_sigmoid_weights.shape, BF16),
            pltpu.VMEM(lookup_content_weights.shape, BF16),
            pltpu.VMEM(attend_final_weights.shape, BF16),
            pltpu.VMEM(outgoing_link_weights.shape, BF16),
            pltpu.VMEM(incoming_link_weights.shape, BF16),
            pltpu.VMEM(trimult_sigmoid_weights.shape, BF16),
            pltpu.VMEM(trimult_final_weights.shape, BF16),
            dma((9,)),
        ]
        + [dma] * 2 + [dma((cols,))] + [dma] * 11,
        compiler_params=pltpu.CompilerParams(
            collective_id=0, has_side_effects=True, vmem_limit_bytes=62 * 2**20
        ),
    )(
        homolog_tensor,
        pairwise_tensor,
        genuine_amino_flags,
        genuine_amino_flags.reshape(1, -1),
        polymer_identity.reshape(1, -1),
        crosspolymer_offset,
        asking_weights,
        attend_sigmoid_weights,
        lookup_content_weights,
        attend_final_weights,
        jnp.transpose(pairwise_logit_weights),
        outgoing_link_weights,
        incoming_link_weights,
        trimult_sigmoid_weights,
        trimult_final_weights,
    )
    return pl.pallas_call(
        deliver,
        out_shape=tuple(jax.ShapeDtypeStruct(r.shape, r.dtype) for r in results),
        in_specs=[hbm, hbm],
        out_specs=(hbm, hbm),
        scratch_shapes=[pltpu.VMEM(r.shape, r.dtype) for r in results] + [dma((5,)), dma((5,))],
        compiler_params=pltpu.CompilerParams(vmem_limit_bytes=62 * 2**20),
    )(*results)


def from_root(array, axis, root):
    mine = lax.axis_index(axis) == root
    return lax.psum(jnp.where(mine, array, jnp.zeros_like(array)), axis)


def standardize_features(tensor):
    tensor = tensor.astype(jnp.float32)
    center = tensor - jnp.mean(tensor, axis=-1, keepdims=True)
    spread = jnp.mean(center * center, axis=-1, keepdims=True)
    return center * lax.rsqrt(spread + 1e-05)


def edges(pair_norm, weight, mask_rows, width):
    projected = jnp.dot(pair_norm, weight, preferred_element_type=jnp.float32)
    edge_vals = (
        mask_rows * jax.nn.sigmoid(projected[..., :width]) * projected[..., width:]
    ).astype(jnp.bfloat16)
    return jnp.transpose(edge_vals, (2, 0, 1))


def local(
    homolog_tensor,
    pairwise_tensor,
    genuine_amino_flags,
    polymer_identity,
    asking_weights,
    attend_sigmoid_weights,
    lookup_content_weights,
    attend_final_weights,
    pairwise_logit_weights,
    crosspolymer_offset,
    outgoing_link_weights,
    incoming_link_weights,
    trimult_sigmoid_weights,
    trimult_final_weights,
):
    row_count = lax.axis_size("row")
    col_count = lax.axis_size("col")
    row_index = lax.axis_index("row")
    col_index = lax.axis_index("col")
    homolog_entries, amino_positions, feature_depth = homolog_tensor.shape
    res_rows = pairwise_tensor.shape[0]
    pair_width = pairwise_tensor.shape[2]
    row_ratio = row_count // col_count
    head_count = pairwise_logit_weights.shape[1]
    inner_width = asking_weights.shape[1]
    per_head_width = inner_width // head_count
    standardized_homologs = standardize_features(homolog_tensor).astype(jnp.bfloat16)
    pair_norm = standardize_features(pairwise_tensor).astype(jnp.bfloat16)
    local_bias = jnp.einsum(
        "ijc,ch->hij", pair_norm, pairwise_logit_weights, preferred_element_type=jnp.float32
    ).astype(jnp.bfloat16)
    row_bias = lax.all_gather(local_bias, "col", axis=2, tiled=True)
    queries = (
        jnp.dot(standardized_homologs, asking_weights, preferred_element_type=jnp.float32)
        * per_head_width ** (-0.5)
    ).astype(jnp.bfloat16)
    queries = queries.reshape(homolog_entries, amino_positions, head_count, per_head_width)
    gate_activation = jax.nn.sigmoid(
        jnp.dot(standardized_homologs, attend_sigmoid_weights, preferred_element_type=jnp.float32)
    )
    all_bias = lax.all_gather(row_bias, "row", axis=1, tiled=True)
    bias_block = lax.dynamic_slice_in_dim(all_bias, col_index * amino_positions, amino_positions, 1)
    query_chain = lax.dynamic_slice_in_dim(
        polymer_identity, col_index * amino_positions, amino_positions, 0
    )
    cross_chain = (query_chain[:, None] != polymer_identity[None, :]).astype(jnp.float32)
    extra_bias = (
        bias_block.astype(jnp.float32) + crosspolymer_offset[:, None, None] * cross_chain[None]
    )
    keep_all = genuine_amino_flags > 0
    key_value = jnp.dot(
        lax.all_gather(standardized_homologs, "col", axis=1, tiled=True),
        lookup_content_weights,
        preferred_element_type=jnp.float32,
    ).astype(jnp.bfloat16)
    piece_len = key_value.shape[1]
    key_rows = key_value[..., :inner_width].reshape(
        homolog_entries, piece_len, head_count, per_head_width
    )
    value_rows = key_value[..., inner_width:].reshape(
        homolog_entries, piece_len, head_count, per_head_width
    )
    scores = jnp.einsum("sqhd,skhd->shqk", queries, key_rows, preferred_element_type=jnp.float32)
    scores = scores + extra_bias[None]
    scores = jnp.where(keep_all, scores, -1000000000.0)
    peak_old = jnp.full((homolog_entries, head_count, amino_positions), -jnp.inf, jnp.float32)
    total_old = jnp.zeros((homolog_entries, head_count, amino_positions), jnp.float32)
    accum_old = jnp.zeros(
        (homolog_entries, head_count, amino_positions, per_head_width), jnp.float32
    )
    peak_now = jnp.max(scores, axis=-1)
    factor = jnp.exp(peak_old - peak_now)
    exp_scores = jnp.exp(scores - peak_now[..., None])
    total_now = total_old * factor + jnp.sum(exp_scores, axis=-1)
    accum_now = accum_old * factor[..., None] + jnp.einsum(
        "shqk,skhd->shqd",
        exp_scores.astype(jnp.bfloat16),
        value_rows,
        preferred_element_type=jnp.float32,
    )
    peak_now, total_now, accum_now = (peak_now, total_now, accum_now)
    attended = accum_now / total_now[..., None]
    attended = jnp.transpose(attended, (0, 2, 1, 3)).reshape(
        homolog_entries, amino_positions, inner_width
    )
    gated_output = (gate_activation * attended).astype(jnp.bfloat16)
    attended_homologs = (
        homolog_tensor.astype(jnp.float32)
        + jnp.dot(gated_output, attend_final_weights, preferred_element_type=jnp.float32)
    ).astype(jnp.bfloat16)
    mask_rows = lax.dynamic_slice_in_dim(
        genuine_amino_flags, row_index * res_rows, res_rows, 0
    ).astype(jnp.float32)[:, None, None]
    left_tri = edges(pair_norm, outgoing_link_weights, mask_rows, pair_width)
    right_tri = edges(pair_norm, incoming_link_weights, mask_rows, pair_width)
    left_cols = lax.all_gather(left_tri, "row", axis=1, tiled=True)
    left_part = lax.dynamic_slice_in_dim(left_cols, row_index % row_ratio * res_rows, res_rows, 2)
    left_mine = from_root(left_part, "col", row_index // row_ratio)
    product = jnp.einsum(
        "cki,ckj->cij",
        left_mine,
        lax.all_gather(right_tri, "row", axis=1, tiled=True),
        preferred_element_type=jnp.float32,
    )
    product_norm = standardize_features(jnp.transpose(product, (1, 2, 0))).astype(jnp.bfloat16)
    tri_gate = jax.nn.sigmoid(
        jnp.dot(pair_norm, trimult_sigmoid_weights, preferred_element_type=jnp.float32)
    )
    update = jnp.dot(product_norm, trimult_final_weights, preferred_element_type=jnp.float32)
    pair_output = (pairwise_tensor.astype(jnp.float32) + tri_gate * update).astype(jnp.bfloat16)
    return (attended_homologs, pair_output)


def solution(mesh):
    in_specs = (
        P("row", "col", None),
        P("row", "col", None),
        P(),
        P(),
        P(),
        P(),
        P(),
        P(),
        P(),
        P(),
        P(),
        P(),
        P(),
        P(),
    )
    out_specs = (P("row", "col", None), P("row", "col", None))

    def local_either(*blocks):
        rows, cols = mesh.shape["row"], mesh.shape["col"]
        homologs, residues, depth = blocks[0].shape
        pair_rows, pair_cols, cz = blocks[1].shape
        heads = blocks[8].shape[1]
        fits = (
            cz == 4 * rows * cols
            and cz == cols * residues
            and cz == rows * pair_rows
            and pair_cols == residues == 32
            and pair_rows == 16
            and heads == 8
            and homologs % (2 * cols) == 0
            and blocks[4].shape[1] == depth
            and depth % 128 == 0
        )
        if fits:
            return local_fused(rows, cols, *blocks)
        return local(*blocks)

    return jax.shard_map(local_either, mesh=mesh, in_specs=in_specs, out_specs=out_specs, check_vma=False)
```
